32 devices in a mesh: pole: 2 (over y), row: 4 (over z), col: 2 (over x), sub: 2 (over core).
Axes of the slice: x: 2, y: 2, z: 4, core: 2. Of those that a mesh axis runs over, the one named last changes fastest.
Arguments:
- parent_inverse: bfloat16 [3072, 1536], P(('pole', 'row'), 'col'), parts along dimension 0, may hold values from -0.15625 to 0.15625
- panel: bfloat16 [48, 1280, 256], P(('pole', 'row'), 'col'), parts along dimension 0, may hold values from -1.1953125 to 1.1953125
- diag_inverse: bfloat16 [48, 256, 256], P(('pole', 'row'), None, 'sub'), parts along dimension 0, may hold values from -6 to 6
- pattern: int32 [24, 5], P('row'), may hold values from 0 to 5, as said below
- widths: int32 [24], P('row'), may hold values from 64 to 256, as said below
Outputs:
- off_block: bfloat16 [48, 1280, 256], P(('pole', 'row'), 'col', 'sub'), parts along dimension 0
- diag_block: bfloat16 [48, 256, 256], P(('pole', 'row'), None, 'sub'), parts along dimension 0
The draws below stay inside these ranges and needn't reach their ends.
There are 2 independent parts, one for each index of `pole`. The reference program is written for one: setup_inputs(seed, part) draws one part's arguments, and reference() takes and returns one part's arrays. A program takes and returns all parts, laid end to end along the dimension named above; an argument that names none is the same for every part. Nothing has to cross between parts.
Inputs may be any that keep to these rules, and one draw needn't show every extreme that they name: `pattern`: each row lists 5 different ancestors in rising order; the last is always the root 6 - 1, and some row names ancestor 0. `widths`: child 0 has the full padded width 256.
All inputs are finite; a program needn't handle non-finite values.
Results may differ from the reference program's by a relative error of at most 0.0045.
Values may be sent and summed in bfloat16 or wider, within the bound.
No kernel may reach another device: no remote copies, remote signals or barrier semaphores. Data moves between devices by JAX's collectives and lax.ppermute only.
A program may use at most 64 MiB of HBM per device.

```python
import jax
import jax.numpy as jnp
from jax import lax

BS = 256
SBLK = 5
NA = 6
CH = 24


def draw_pattern(key, part):
    key = jax.random.fold_in(key, 11)
    child_keys = jax.random.split(key, CH)

    def one_row(row_key):
        order = jax.random.permutation(row_key, NA - 1)
        return jnp.sort(order[:SBLK - 1])
    others = jax.vmap(one_row)(child_keys)
    others = others.at[0, 0].set(0)
    root_col = jnp.full((CH, 1), NA - 1, dtype=jnp.int32)
    return jnp.concatenate([others.astype(jnp.int32), root_col], axis=1).astype(jnp.int32)


def draw_widths(key, part):
    key = jax.random.fold_in(key, 23)
    values = jax.random.randint(key, (CH,), BS // 4, BS + 1)
    values = values.at[0].set(BS)
    values = values.at[1].set(BS // 4)
    return values.astype(jnp.int32)


def steps_of(key, dims, pieces, least, top_value):
    loudness, own = 1.0, jax.random.fold_in(key, 6)
    for dim, shards_of in pieces:
        draws = jnp.exp(jax.random.uniform(jax.random.fold_in(own, dim), (shards_of,), jnp.float32, least / len(pieces), top_value / len(pieces)))
        loudness = loudness * jnp.repeat(draws, dims[dim] // shards_of).reshape([-1 if axis == dim else 1 for axis in range(len(dims))])
    return loudness


def normal_values(rng, shape, spread, most, shards=(), held_as=jnp.bfloat16):
    values = jax.random.normal(rng, shape, jnp.float32) * spread
    if len(shards) > 0:
        values = steps_of(rng, shape, shards, -0.22, 0.18) * values
    return jnp.clip(values, min=-most, max=most).astype(held_as)


def setup_inputs(seed: int = 0, part: int = 0) -> dict:
    key_of = jax.random.split(jax.random.key(seed), 6)
    part_keys = jax.random.split(jax.random.fold_in(key_of[5], part), 6)
    return {
        "parent_inverse": normal_values(part_keys[0], (NA * BS, NA * BS), (SBLK * BS) ** -0.5, 0.15625, ((0, 4), (1, 2))),
        "panel": normal_values(part_keys[1], (CH, SBLK * BS, BS), 0.2, 1.1953125, ((0, 4), (1, 2))),
        "diag_inverse": normal_values(part_keys[2], (CH, BS, BS), 1.0, 6.0, ((0, 4), (2, 2))),
        "pattern": draw_pattern(jax.random.fold_in(key_of[5], 71), part),
        "widths": draw_widths(jax.random.fold_in(key_of[5], 71), part),
    }


def reference(parent_inverse, panel, diag_inverse, pattern, widths):
    col_mask = jnp.arange(BS)[None, :] < widths[:, None]
    masked = panel * col_mask[:, None, :].astype(jnp.bfloat16)
    blocks_all = parent_inverse.reshape(NA, BS, NA, BS)

    def one_child(child_items):
        chosen, slab_cols = child_items
        picked = jnp.take(blocks_all, chosen, axis=0)
        picked = jnp.take(picked, chosen, axis=2).reshape(SBLK * BS, SBLK * BS)
        product = jnp.dot(picked, slab_cols, preferred_element_type=jnp.float32)
        return (-product).astype(jnp.bfloat16)

    off_block = lax.map(one_child, (pattern.astype(jnp.int32), masked))
    diag_terms = jnp.einsum("jrb,jrc->jbc", masked.astype(jnp.float32), off_block.astype(jnp.float32))
    diag_mask = (col_mask[:, :, None] & col_mask[:, None, :]).astype(jnp.float32)
    diag_block = (diag_inverse.astype(jnp.float32) * diag_mask - diag_terms).astype(jnp.bfloat16)
    return off_block, diag_block
```

```python
import functools

import jax
import jax.numpy as jnp
from jax import lax
from jax.experimental import pallas as pl
from jax.experimental.pallas import tpu as pltpu
from jax.sharding import PartitionSpec as P

SWAP = [(0, 1), (1, 0)]
F32 = jnp.float32
BF16 = jnp.bfloat16


def generic(parent_inverse, panel, diag_inverse, pattern, widths):
    block_size = panel.shape[2]
    half_cols = block_size // lax.axis_size("sub")
    sub_idx = lax.axis_index("sub")
    col_idx = lax.axis_index("col")
    col_mask = jnp.arange(block_size)[None, :] < widths[:, None]
    masked = panel * col_mask[:, None, :].astype(BF16)
    half_panel = lax.dynamic_slice_in_dim(masked, sub_idx * half_cols, half_cols, 2)
    full_panel = lax.all_gather(half_panel, "col", axis=1, tiled=True)
    columns = lax.all_gather(parent_inverse, "row", axis=0, tiled=True)
    pat_blocks = pattern.shape[1]
    local_blocks = columns.shape[1] // block_size
    anc_count = columns.shape[0] // block_size
    blocks_all = columns.reshape(anc_count, block_size, columns.shape[1])
    owned_ids = col_idx * local_blocks + jnp.arange(local_blocks, dtype=jnp.int32)

    def one_child(child_items):
        chosen, slab_cols = child_items
        sel_rows = jnp.take(blocks_all, chosen, axis=0).reshape(pat_blocks * block_size, columns.shape[1])
        onehot = (owned_ids[:, None] == chosen[None, :]).astype(BF16)
        slab = slab_cols.reshape(pat_blocks, block_size, half_cols)
        placed = jnp.einsum("km,mbc->kbc", onehot, slab, preferred_element_type=F32)
        placed = placed.astype(BF16).reshape(local_blocks * block_size, half_cols)
        return jnp.dot(sel_rows, placed, preferred_element_type=F32)

    partial_value = lax.map(one_child, (pattern, full_panel))
    summed = lax.psum_scatter(partial_value, "col", scatter_dimension=1, tiled=True)
    off_block = (-summed).astype(BF16)
    diag_terms = jnp.einsum("jrb,jrc->jbc", masked, off_block, preferred_element_type=F32)
    diag_total = lax.psum(diag_terms, "col")
    mask_half = lax.dynamic_slice_in_dim(col_mask, sub_idx * half_cols, half_cols, 1)
    diag_mask = (col_mask[:, :, None] & mask_half[:, None, :]).astype(F32)
    diag_block = (diag_inverse.astype(F32) * diag_mask - diag_total).astype(BF16)
    return (off_block, diag_block)


def spread_kernel(ids, pat, mine, other, out):
    children, rows, width = mine.shape
    c = ids[1]
    blocks = out.shape[0] // 256
    per_col = blocks // 2
    chunks = rows // 128
    out[...] = jnp.zeros_like(out)
    for who, src in ((c, mine), (1 - c, other)):
        for j in range(children):
            for q in range(chunks):
                g = who * chunks + q
                anc = pat[j, g // 2]
                side = jnp.where(anc // per_col == c, 0, per_col)
                start = (side + anc % per_col) * 256 + (g % 2) * 128
                out[pl.ds(pl.multiple_of(start, 128), 128), j * width : (j + 1) * width] = src[
                    j, q * 128 : (q + 1) * 128, :
                ]


def product_kernel(a0, a1, b0, b1, spread, out, rows):
    half, wide = a0.shape
    rows[:half, :wide] = a0[...]
    rows[half:, :wide] = a1[...]
    rows[:half, wide:] = b0[...]
    rows[half:, wide:] = b1[...]
    out[...] = (-jnp.dot(rows[...], spread[...], preferred_element_type=F32)).astype(BF16)


def final_kernel(ids, pat, widths, y0, y1, y2, y3, panel, same, cross, dinv, off_out, diag_out, full, off):
    j = pl.program_id(0)
    r, c, s = ids[0], ids[1], ids[2]
    _, rows, width = panel.shape
    half = y0.shape[0] // 2
    lane = y0.shape[1] // pl.num_programs(0)

    @pl.when(j == 0)
    def _():
        for k, y in enumerate((y0, y1, y2, y3)):
            shard = jnp.bitwise_xor(r, k)
            for side in range(2):
                where = jnp.where(s == side, 0, half)
                full[pl.ds(pl.multiple_of(shard * 2 * half + side * half, 64), half), :] = y[
                    pl.ds(pl.multiple_of(where, 64), half), :
                ]

    col = pl.ds(pl.multiple_of(j * lane, 128), lane)
    chunks = rows // 128
    for n, who in enumerate((c, 1 - c)):
        for q in range(chunks):
            g = who * chunks + q
            start = pat[j, g // 2] * 256 + (g % 2) * 128
            off[n * rows + q * 128 : n * rows + (q + 1) * 128, :] = full[
                pl.ds(pl.multiple_of(start, 128), 128), col
            ]
    w = widths[j]
    keep_b = s * lane + lax.broadcasted_iota(jnp.int32, (1, lane), 1) < w
    keep_a = lax.broadcasted_iota(jnp.int32, (width, 1), 0) < w
    own = off[:rows, :]
    off_out[0] = jnp.where(keep_b, own, jnp.zeros_like(own))
    dims = (((0,), (0,)), ((), ()))
    terms = lax.dot_general(panel[j], own, dims, preferred_element_type=F32)
    oth = off[rows:, :]
    t_same = lax.dot_general(same[j], oth, dims, preferred_element_type=F32)
    t_cross = lax.dot_general(cross[j], oth, dims, preferred_element_type=F32)
    low = jnp.where(s == 0, t_same, t_cross)
    high = jnp.where(s == 0, t_cross, t_same)
    terms = terms + jnp.concatenate([low, high], axis=0)
    diag = dinv[0].astype(F32) - terms
    diag_out[0] = jnp.where(keep_a & keep_b, diag, 0.0).astype(BF16)


VMEM = pl.BlockSpec(memory_space=pltpu.VMEM)
SMEM = pl.BlockSpec(memory_space=pltpu.SMEM)


def gathered(parent, panel, diag_inverse, pattern, widths):
    r, c, s = lax.axis_index("row"), lax.axis_index("col"), lax.axis_index("sub")
    children, rows, width = panel.shape
    lane = width // 2
    half, wide = parent.shape[0] // 2, parent.shape[1]
    ids = jnp.stack([r, c, s]).astype(jnp.int32)

    def xor(d):
        return [(i, i ^ d) for i in range(4)]

    def sib(x):
        return lax.ppermute(x, "sub", SWAP)

    own = lax.dynamic_slice_in_dim(parent, s * half, half, 0)
    own_sib = lax.dynamic_slice_in_dim(parent, (1 - s) * half, half, 0)
    mine = lax.dynamic_slice_in_dim(panel, s * lane, lane, 2)
    b0 = lax.ppermute(own, "col", SWAP)
    same = lax.ppermute(mine, "col", SWAP)
    a1, a2, a3 = (lax.ppermute(own, "row", xor(d)) for d in (1, 2, 3))
    b1 = lax.ppermute(b0, "row", xor(1))
    cut = half // 2
    b2 = jnp.concatenate(
        [lax.ppermute(b0[:cut], "row", xor(2)), lax.ppermute(a2[cut:], "col", SWAP)], axis=0
    )
    b3 = lax.ppermute(a3, "col", SWAP)
    cross = sib(same)

    spread = pl.pallas_call(
        spread_kernel,
        out_shape=jax.ShapeDtypeStruct((2 * wide, children * lane), BF16),
        in_specs=[SMEM, SMEM, VMEM, VMEM],
        out_specs=VMEM,
        cost_estimate=pl.CostEstimate(flops=0, bytes_accessed=4 << 20, transcendentals=0),
        name="spread",
    )(ids, pattern, mine, same)

    product = pl.pallas_call(
        product_kernel,
        out_shape=jax.ShapeDtypeStruct((2 * half, children * lane), BF16),
        in_specs=[VMEM] * 5,
        out_specs=VMEM,
        scratch_shapes=[pltpu.VMEM((2 * half, 2 * wide), BF16)],
        cost_estimate=pl.CostEstimate(
            flops=2 * 2 * half * 2 * wide * children * lane, bytes_accessed=4 << 20, transcendentals=0
        ),
        compiler_params=pltpu.CompilerParams(vmem_limit_bytes=24 << 20),
        name="product",
    )
    ys = [
        product(own, own_sib, b0, sib(b0), spread),
        product(a1, sib(a1), b1, sib(b1), spread),
        product(a2, sib(a2), b2, sib(b2), spread),
        product(a3, sib(a3), b3, sib(b3), spread),
    ]
    return pl.pallas_call(
        final_kernel,
        grid=(children,),
        out_shape=(
            jax.ShapeDtypeStruct((children, rows, lane), BF16),
            jax.ShapeDtypeStruct((children, width, lane), BF16),
        ),
        in_specs=[SMEM, SMEM, SMEM] + [VMEM] * 7 + [pl.BlockSpec((1, width, lane), lambda j: (j, 0, 0))],
        out_specs=(
            pl.BlockSpec((1, rows, lane), lambda j: (j, 0, 0)),
            pl.BlockSpec((1, width, lane), lambda j: (j, 0, 0)),
        ),
        scratch_shapes=[
            pltpu.VMEM((4 * 2 * half, children * lane), BF16),
            pltpu.VMEM((2 * rows, lane), BF16),
        ],
        cost_estimate=pl.CostEstimate(
            flops=2 * children * width * 2 * rows * lane, bytes_accessed=8 << 20, transcendentals=0
        ),
        compiler_params=pltpu.CompilerParams(vmem_limit_bytes=24 << 20),
        name="final",
    )(ids, pattern, widths, *ys, panel, same, cross, diag_inverse)


def solution(mesh):
    placed = (
        P(("pole", "row"), "col"),
        P(("pole", "row"), "col", None),
        P(("pole", "row"), None, "sub"),
        P("row", None),
        P("row"),
    )
    shape = dict(mesh.shape)
    fits = (shape["row"], shape["col"], shape["sub"]) == (4, 2, 2)
    return jax.shard_map(
        gathered if fits else generic,
        mesh=mesh,
        in_specs=placed,
        out_specs=(P(("pole", "row"), "col", "sub"), P(("pole", "row"), None, "sub")),
        check_vma=False,
    )
```

```python
import jax
import jax.numpy as jnp
from jax import lax
from jax.experimental import pallas as pl
from jax.experimental.pallas import tpu as pltpu
from jax.sharding import PartitionSpec as P

SWAP = [(0, 1), (1, 0)]
F32 = jnp.float32
BF16 = jnp.bfloat16


def generic(parent_inverse, panel, diag_inverse, pattern, widths):
    block_size = panel.shape[2]
    half_cols = block_size // lax.axis_size("sub")
    sub_idx = lax.axis_index("sub")
    col_idx = lax.axis_index("col")
    col_mask = jnp.arange(block_size)[None, :] < widths[:, None]
    masked = panel * col_mask[:, None, :].astype(BF16)
    half_panel = lax.dynamic_slice_in_dim(masked, sub_idx * half_cols, half_cols, 2)
    full_panel = lax.all_gather(half_panel, "col", axis=1, tiled=True)
    columns = lax.all_gather(parent_inverse, "row", axis=0, tiled=True)
    pat_blocks = pattern.shape[1]
    local_blocks = columns.shape[1] // block_size
    anc_count = columns.shape[0] // block_size
    blocks_all = columns.reshape(anc_count, block_size, columns.shape[1])
    owned_ids = col_idx * local_blocks + jnp.arange(local_blocks, dtype=jnp.int32)

    def one_child(child_items):
        chosen, slab_cols = child_items
        sel_rows = jnp.take(blocks_all, chosen, axis=0).reshape(pat_blocks * block_size, columns.shape[1])
        onehot = (owned_ids[:, None] == chosen[None, :]).astype(BF16)
        slab = slab_cols.reshape(pat_blocks, block_size, half_cols)
        placed = jnp.einsum("km,mbc->kbc", onehot, slab, preferred_element_type=F32)
        placed = placed.astype(BF16).reshape(local_blocks * block_size, half_cols)
        return jnp.dot(sel_rows, placed, preferred_element_type=F32)

    partial_value = lax.map(one_child, (pattern, full_panel))
    summed = lax.psum_scatter(partial_value, "col", scatter_dimension=1, tiled=True)
    off_block = (-summed).astype(BF16)
    diag_terms = jnp.einsum("jrb,jrc->jbc", masked, off_block, preferred_element_type=F32)
    diag_total = lax.psum(diag_terms, "col")
    mask_half = lax.dynamic_slice_in_dim(col_mask, sub_idx * half_cols, half_cols, 1)
    diag_mask = (col_mask[:, :, None] & mask_half[:, None, :]).astype(F32)
    diag_block = (diag_inverse.astype(F32) * diag_mask - diag_total).astype(BF16)
    return (off_block, diag_block)


def pack_kernel(ids, parent, panel, tile, half_panel, sems):
    s = ids[2]
    half, lane = tile.shape[0], half_panel.shape[2]
    copies = [
        pltpu.make_async_copy(parent.at[pl.ds(pl.multiple_of(s * half, 64), half), :], tile, sems.at[0]),
        pltpu.make_async_copy(panel.at[:, :, pl.ds(pl.multiple_of(s * lane, 128), lane)], half_panel, sems.at[1]),
    ]
    for copy in copies:
        copy.start()
    for copy in copies:
        copy.wait()


def spread_kernel(ids, pat, panel, same, cross, out, full):
    children, rows, width = panel.shape
    lane = width // 2
    c, s = ids[1], ids[2]
    blocks = out.shape[0] // width
    per_col = blocks // 2
    chunks = rows // 128
    low = pl.ds(pl.multiple_of(s * lane, 128), lane)
    out[...] = jnp.zeros_like(out)
    full[...] = jnp.zeros_like(full)
    for j in range(children):
        for q in range(2 * chunks):
            g = (c if q < chunks else 1 - c) * chunks + q % chunks
            anc = pat[j, g // 2]
            side = jnp.where(anc // per_col == c, 0, per_col)
            start = (side + anc % per_col) * width + (g % 2) * 128
            here = pl.ds(pl.multiple_of(start, 128), 128)
            band = slice(q % chunks * 128, (q % chunks + 1) * 128)
            mine = slice(j * lane, (j + 1) * lane)
            if q < chunks:
                out[here, mine] = panel[j, band, low]
                full[here, j * width : (j + 1) * width] = panel[j, band, :]
            else:
                block = same[j, band, :]
                out[here, mine] = block
                full[here, pl.ds(pl.multiple_of(j * width + s * lane, 128), lane)] = block
                full[here, pl.ds(pl.multiple_of(j * width + (1 - s) * lane, 128), lane)] = cross[j, band, :]


def halves(ids, half):
    s = ids[2]
    return [pl.ds(pl.multiple_of(side * half, 64), half) for side in (s, 1 - s)]


def early_kernel(ids, parent, a, a_sib, spread, y0, acc, rows):
    tall, wide = parent.shape
    half = tall // 2
    own, sib = halves(ids, half)
    rows[:, :wide] = parent[...]
    for here, piece in ((own, a), (sib, a_sib)):
        rows[here, wide:] = piece[:half, :]
    y0[...] = (-jnp.dot(rows[...], spread[...], preferred_element_type=F32)).astype(BF16)
    for k in range(1, 4):
        for here, piece in ((own, a), (sib, a_sib)):
            rows[here, :wide] = piece[k * half : (k + 1) * half, :]
        acc[(k - 1) * tall : k * tall, :] = jnp.dot(rows[:, :wide], spread[:wide, :], preferred_element_type=F32)


def final_kernel(ids, pat, widths, b, b_sib, spread, full, y0, acc, dinv, off_out, diag_out, rows, y_all):
    r, c, s = ids[0], ids[1], ids[2]
    children, width, lane = dinv.shape
    tall, wide = rows.shape
    half = tall // 2
    total = y_all.shape[0]
    own, sib = halves(ids, half)

    def place(k, y):
        at = lax.rem(jnp.bitwise_xor(r, k) * tall + c * wide, total)
        y_all[pl.ds(pl.multiple_of(at, 128), tall), :] = y

    place(0, y0[...])
    for k in range(1, 4):
        for here, piece in ((own, b), (sib, b_sib)):
            rows[here, :] = piece[(k - 1) * half : k * half, :]
        term = jnp.dot(rows[...], spread[wide:, :], preferred_element_type=F32)
        place(k, (-(acc[(k - 1) * tall : k * tall, :] + term)).astype(BF16))
    chunks = off_out.shape[1] // 128
    for j in range(children):
        w = widths[j]
        mine = slice(j * lane, (j + 1) * lane)
        keep_b = s * lane + lax.broadcasted_iota(jnp.int32, (1, lane), 1) < w
        keep_a = lax.broadcasted_iota(jnp.int32, (width, 1), 0) < w
        for q in range(chunks):
            g = c * chunks + q
            start = lax.rem(pat[j, g // 2] * width + (g % 2) * 128 + c * wide, total)
            got = y_all[pl.ds(pl.multiple_of(start, 128), 128), mine]
            off_out[j, q * 128 : (q + 1) * 128, :] = jnp.where(keep_b, got, jnp.zeros_like(got))
        terms = lax.dot_general(
            y_all[:, mine], full[:, j * width : (j + 1) * width], (((0,), (0,)), ((), ())), preferred_element_type=F32
        )
        diag = dinv[j].astype(F32) - terms.T
        diag_out[j] = jnp.where(keep_a & keep_b, diag, 0.0).astype(BF16)


VMEM = pl.BlockSpec(memory_space=pltpu.VMEM)
SMEM = pl.BlockSpec(memory_space=pltpu.SMEM)
ANY = pl.BlockSpec(memory_space=pl.ANY)
FREE = pl.CostEstimate(flops=0, bytes_accessed=0, transcendentals=0)


def gathered(parent, panel, diag_inverse, pattern, widths):
    r, c, s = lax.axis_index("row"), lax.axis_index("col"), lax.axis_index("sub")
    children, rows, width = panel.shape
    lane = width // 2
    tall, wide = parent.shape
    half = tall // 2
    lanes = children * lane
    ids = jnp.stack([r, c, s]).astype(jnp.int32)

    def xor(d):
        return [(i, i ^ d) for i in range(4)]

    def sib(x):
        return lax.ppermute(x, "sub", SWAP)

    def params(mib):
        return pltpu.CompilerParams(vmem_limit_bytes=mib << 20)

    tile, mine = pl.pallas_call(
        pack_kernel,
        out_shape=(
            jax.ShapeDtypeStruct((half, wide), BF16),
            jax.ShapeDtypeStruct((children, rows, lane), BF16),
        ),
        in_specs=[SMEM, ANY, ANY],
        out_specs=(VMEM, VMEM),
        scratch_shapes=[pltpu.SemaphoreType.DMA((2,))],
        cost_estimate=FREE,
        compiler_params=params(8),
        name="pack",
    )(ids, parent, panel)
    a1, a2, a3 = (lax.ppermute(tile, "row", xor(d)) for d in (1, 2, 3))
    b0 = lax.ppermute(tile, "col", SWAP)
    same = lax.ppermute(mine, "col", SWAP)
    a1, a2, a3, b0 = lax.optimization_barrier((a1, a2, a3, b0))
    cut = half // 2
    b1 = lax.ppermute(b0, "row", xor(1))
    b3z = lax.ppermute(b0[:cut], "row", xor(3))
    b23 = lax.ppermute(jnp.concatenate([a2, a3[cut:]]), "col", SWAP)
    a = jnp.concatenate([b0, a1, a2, a3])
    a_sib = sib(a)
    cross = sib(same)

    spread, full = pl.pallas_call(
        spread_kernel,
        out_shape=(
            jax.ShapeDtypeStruct((2 * wide, lanes), BF16),
            jax.ShapeDtypeStruct((2 * wide, 2 * lanes), BF16),
        ),
        in_specs=[SMEM, SMEM] + [VMEM] * 3,
        out_specs=(VMEM, VMEM),
        cost_estimate=FREE,
        compiler_params=params(12),
        name="spread",
    )(ids, pattern, panel, same, cross)
    y0, acc = pl.pallas_call(
        early_kernel,
        out_shape=(
            jax.ShapeDtypeStruct((tall, lanes), BF16),
            jax.ShapeDtypeStruct((3 * tall, lanes), F32),
        ),
        in_specs=[SMEM] + [VMEM] * 4,
        out_specs=(VMEM, VMEM),
        scratch_shapes=[pltpu.VMEM((tall, 2 * wide), BF16)],
        cost_estimate=FREE,
        compiler_params=params(12),
        name="early",
    )(ids, parent, a, a_sib, spread)
    b1, b3z, b23, y0, acc = lax.optimization_barrier((b1, b3z, b23, y0, acc))
    b = jnp.concatenate([b1, b23[:half], b3z, b23[half:]])
    b_sib = sib(b)
    return pl.pallas_call(
        final_kernel,
        out_shape=(
            jax.ShapeDtypeStruct((children, rows, lane), BF16),
            jax.ShapeDtypeStruct((children, width, lane), BF16),
        ),
        in_specs=[SMEM, SMEM, SMEM] + [VMEM] * 7,
        out_specs=(VMEM, VMEM),
        scratch_shapes=[
            pltpu.VMEM((tall, wide), BF16),
            pltpu.VMEM((4 * tall, lanes), BF16),
        ],
        cost_estimate=FREE,
        compiler_params=params(16),
        name="final",
    )(ids, pattern, widths, b, b_sib, spread, full, y0, acc, diag_inverse)


def solution(mesh):
    placed = (
        P(("pole", "row"), "col"),
        P(("pole", "row"), "col", None),
        P(("pole", "row"), None, "sub"),
        P("row", None),
        P("row"),
    )
    shape = dict(mesh.shape)
    fits = (shape["row"], shape["col"], shape["sub"]) == (4, 2, 2)
    return jax.shard_map(
        gathered if fits else generic,
        mesh=mesh,
        in_specs=placed,
        out_specs=(P(("pole", "row"), "col", "sub"), P(("pole", "row"), None, "sub")),
        check_vma=False,
    )
```

```python
import jax
import jax.numpy as jnp
from jax import lax
from jax.experimental import pallas as pl
from jax.experimental.pallas import tpu as pltpu
from jax.sharding import PartitionSpec as P

SWAP = [(0, 1), (1, 0)]
F32 = jnp.float32
BF16 = jnp.bfloat16


def generic(parent_inverse, panel, diag_inverse, pattern, widths):
    block_size = panel.shape[2]
    half_cols = block_size // lax.axis_size("sub")
    sub_idx = lax.axis_index("sub")
    col_idx = lax.axis_index("col")
    col_mask = jnp.arange(block_size)[None, :] < widths[:, None]
    masked = panel * col_mask[:, None, :].astype(BF16)
    half_panel = lax.dynamic_slice_in_dim(masked, sub_idx * half_cols, half_cols, 2)
    full_panel = lax.all_gather(half_panel, "col", axis=1, tiled=True)
    columns = lax.all_gather(parent_inverse, "row", axis=0, tiled=True)
    pat_blocks = pattern.shape[1]
    local_blocks = columns.shape[1] // block_size
    anc_count = columns.shape[0] // block_size
    blocks_all = columns.reshape(anc_count, block_size, columns.shape[1])
    owned_ids = col_idx * local_blocks + jnp.arange(local_blocks, dtype=jnp.int32)

    def one_child(child_items):
        chosen, slab_cols = child_items
        sel_rows = jnp.take(blocks_all, chosen, axis=0).reshape(pat_blocks * block_size, columns.shape[1])
        onehot = (owned_ids[:, None] == chosen[None, :]).astype(BF16)
        slab = slab_cols.reshape(pat_blocks, block_size, half_cols)
        placed = jnp.einsum("km,mbc->kbc", onehot, slab, preferred_element_type=F32)
        placed = placed.astype(BF16).reshape(local_blocks * block_size, half_cols)
        return jnp.dot(sel_rows, placed, preferred_element_type=F32)

    partial_value = lax.map(one_child, (pattern, full_panel))
    summed = lax.psum_scatter(partial_value, "col", scatter_dimension=1, tiled=True)
    off_block = (-summed).astype(BF16)
    diag_terms = jnp.einsum("jrb,jrc->jbc", masked, off_block, preferred_element_type=F32)
    diag_total = lax.psum(diag_terms, "col")
    mask_half = lax.dynamic_slice_in_dim(col_mask, sub_idx * half_cols, half_cols, 1)
    diag_mask = (col_mask[:, :, None] & mask_half[:, None, :]).astype(F32)
    diag_block = (diag_inverse.astype(F32) * diag_mask - diag_total).astype(BF16)
    return (off_block, diag_block)


def places(ids, pat, blocks, width, children, chunks):
    c = ids[1]
    per_col = blocks // 2
    for j in range(children):
        for q in range(2 * chunks):
            g = (c if q < chunks else 1 - c) * chunks + q % chunks
            anc = pat[j, g // 2]
            side = jnp.where(anc // per_col == c, 0, per_col)
            start = (side + anc % per_col) * width + (g % 2) * 128
            yield j, q, pl.ds(pl.multiple_of(start, 128), 128)


def spread_kernel(ids, pat, panel, same, out):
    children, rows, width = panel.shape
    lane = width // 2
    chunks = rows // 128
    low = pl.ds(pl.multiple_of(ids[2] * lane, 128), lane)
    out[...] = jnp.zeros_like(out)
    for j, q, here in places(ids, pat, out.shape[0] // width, width, children, chunks):
        mine = slice(j * lane, (j + 1) * lane)
        band = slice(q % chunks * 128, (q % chunks + 1) * 128)
        if q < chunks:
            out[here, mine] = panel[j, band, low]
        else:
            out[here, mine] = same[j, band, :]


def widen_kernel(ids, pat, panel, same, *refs):
    *cross, out = refs
    children, rows, width = panel.shape
    lane = width // 2
    s = ids[2]
    chunks = rows // 128
    out[...] = jnp.zeros_like(out)
    for j, q, here in places(ids, pat, out.shape[0] // width, width, children, chunks):
        band = slice(q % chunks * 128, (q % chunks + 1) * 128)
        if q < chunks:
            out[here, j * width : (j + 1) * width] = panel[j, band, :]
        else:
            part, at = divmod(j, cross[0].shape[0])
            out[here, pl.ds(pl.multiple_of(j * width + s * lane, 128), lane)] = same[j, band, :]
            out[here, pl.ds(pl.multiple_of(j * width + (1 - s) * lane, 128), lane)] = cross[part][at, band, :]


def pick(s, out, first, second):
    @pl.when(s == 0)
    def _():
        out[...] = first[...]

    @pl.when(s == 1)
    def _():
        out[...] = second[...]


def early_kernel(ids, parent, z1, z1_sib, z2, z2_sib, spread, y0, acc, rows):
    s = ids[2]
    tall, wide = parent.shape
    rows[:, :wide] = parent[...]
    pick(s, rows.at[:, wide:], z2_sib, z2)
    y0[...] = (-jnp.dot(rows[...], spread[...], preferred_element_type=F32)).astype(BF16)
    for k, first, second in ((1, z1_sib, z1), (2, z2, z2_sib), (3, z1, z1_sib)):
        pick(s, rows.at[:, :wide], first, second)
        acc[(k - 1) * tall : k * tall, :] = jnp.dot(rows[:, :wide], spread[:wide, :], preferred_element_type=F32)


def final_kernel(
    ids, pat, widths, q1, q1_sib, q2, q2_sib, spread, full, y0, acc, dinv, off_out, diag_out, rows, y_all
):
    r, c, s = ids[0], ids[1], ids[2]
    children, width, lane = dinv.shape
    tall, wide = rows.shape
    total = y_all.shape[0]

    def place(k, y):
        at = lax.rem(jnp.bitwise_xor(r, k) * tall + c * wide, total)
        y_all[pl.ds(pl.multiple_of(at, 128), tall), :] = y

    place(0, y0[...])
    cut = q2.shape[0]
    for k, first, second in ((1, q1_sib, q1), (2, q1, q1_sib), (3, q2_sib, q2)):
        if k < 3:
            pick(s, rows, first, second)
        else:
            pick(s, rows.at[:cut, :], first, second)
            pick(s, rows.at[cut:, :], second, first)
        term = jnp.dot(rows[...], spread[wide:, :], preferred_element_type=F32)
        place(k, (-(acc[(k - 1) * tall : k * tall, :] + term)).astype(BF16))
    chunks = off_out.shape[1] // 128
    for j in range(children):
        w = widths[j]
        mine = slice(j * lane, (j + 1) * lane)
        keep_b = s * lane + lax.broadcasted_iota(jnp.int32, (1, lane), 1) < w
        keep_a = lax.broadcasted_iota(jnp.int32, (width, 1), 0) < w
        for q in range(chunks):
            g = c * chunks + q
            start = lax.rem(pat[j, g // 2] * width + (g % 2) * 128 + c * wide, total)
            got = y_all[pl.ds(pl.multiple_of(start, 128), 128), mine]
            off_out[j, q * 128 : (q + 1) * 128, :] = jnp.where(keep_b, got, jnp.zeros_like(got))
        terms = lax.dot_general(
            y_all[:, mine], full[:, j * width : (j + 1) * width], (((0,), (0,)), ((), ())), preferred_element_type=F32
        )
        diag = dinv[j].astype(F32) - terms.T
        diag_out[j] = jnp.where(keep_a & keep_b, diag, 0.0).astype(BF16)


VMEM = pl.BlockSpec(memory_space=pltpu.VMEM)
SMEM = pl.BlockSpec(memory_space=pltpu.SMEM)


def cost(flops):
    return pl.CostEstimate(flops=flops, bytes_accessed=0, transcendentals=0)


FREE = cost(0)


def gathered(parent, panel, diag_inverse, pattern, widths):
    r, c, s = lax.axis_index("row"), lax.axis_index("col"), lax.axis_index("sub")
    children, rows, width = panel.shape
    lane = width // 2
    tall, wide = parent.shape
    lanes = children * lane
    ids = jnp.stack([r, c, s]).astype(jnp.int32)

    def core(first, second):
        pairs = []
        for row in range(4):
            for col in range(2):
                for sub, to in enumerate((first, second)):
                    if to is not None:
                        to_row, to_col = to(row, col)
                        pairs.append(((row * 2 + col) * 2 + sub, (to_row * 2 + to_col) * 2 + sub))
        return pairs

    def along(d):
        return lambda row, col: (row ^ d, col)

    def across(row, col):
        return row, 1 - col

    def send(x, first, second):
        return lax.ppermute(x, ("row", "col", "sub"), core(first, second))

    def sib(x):
        return lax.ppermute(x, "sub", SWAP)

    def params(mib):
        return pltpu.CompilerParams(vmem_limit_bytes=mib << 20)

    z1 = send(parent, along(3), along(1))
    z2 = send(parent, along(2), across)
    mine = lax.dynamic_slice_in_dim(panel, s * lane, lane, 2)
    same = lax.ppermute(mine, "col", SWAP)
    q1 = send(z2, across, along(1))
    cut = tall // 2
    q2 = send(jnp.where(s == 0, z1[cut:], z2[:cut]), across, along(3))
    cross = [sib(same[: children // 2]), sib(same[children // 2 :])]

    spread = pl.pallas_call(
        spread_kernel,
        out_shape=jax.ShapeDtypeStruct((2 * wide, lanes), BF16),
        in_specs=[SMEM, SMEM] + [VMEM] * 2,
        out_specs=VMEM,
        cost_estimate=cost(500000000),
        compiler_params=params(8),
        name="spread",
    )(ids, pattern, panel, same)
    full = pl.pallas_call(
        widen_kernel,
        out_shape=jax.ShapeDtypeStruct((2 * wide, 2 * lanes), BF16),
        in_specs=[SMEM, SMEM] + [VMEM] * 4,
        out_specs=VMEM,
        cost_estimate=FREE,
        compiler_params=params(8),
        name="widen",
    )(ids, pattern, panel, same, *cross)
    y0, acc = pl.pallas_call(
        early_kernel,
        out_shape=(
            jax.ShapeDtypeStruct((tall, lanes), BF16),
            jax.ShapeDtypeStruct((3 * tall, lanes), F32),
        ),
        in_specs=[SMEM] + [VMEM] * 6,
        out_specs=(VMEM, VMEM),
        scratch_shapes=[pltpu.VMEM((tall, 2 * wide), BF16)],
        cost_estimate=cost(800000000),
        compiler_params=params(12),
        name="early",
    )(ids, parent, z1, sib(z1), z2, sib(z2), spread)
    q2, y0, acc = lax.optimization_barrier((q2, y0, acc))
    return pl.pallas_call(
        final_kernel,
        out_shape=(
            jax.ShapeDtypeStruct((children, rows, lane), BF16),
            jax.ShapeDtypeStruct((children, width, lane), BF16),
        ),
        in_specs=[SMEM, SMEM, SMEM] + [VMEM] * 9,
        out_specs=(VMEM, VMEM),
        scratch_shapes=[
            pltpu.VMEM((tall, wide), BF16),
            pltpu.VMEM((4 * tall, lanes), BF16),
        ],
        cost_estimate=FREE,
        compiler_params=params(16),
        name="final",
    )(ids, pattern, widths, q1, sib(q1), q2, sib(q2), spread, full, y0, acc, diag_inverse)


def solution(mesh):
    placed = (
        P(("pole", "row"), "col"),
        P(("pole", "row"), "col", None),
        P(("pole", "row"), None, "sub"),
        P("row", None),
        P("row"),
    )
    shape = dict(mesh.shape)
    fits = (shape["row"], shape["col"], shape["sub"]) == (4, 2, 2)
    return jax.shard_map(
        gathered if fits else generic,
        mesh=mesh,
        in_specs=placed,
        out_specs=(P(("pole", "row"), "col", "sub"), P(("pole", "row"), None, "sub")),
        check_vma=False,
    )
```

```python
import jax
import jax.numpy as jnp
from jax import lax
from jax.experimental import pallas as pl
from jax.experimental.pallas import tpu as pltpu
from jax.sharding import PartitionSpec as P

SWAP = [(0, 1), (1, 0)]
F32 = jnp.float32
BF16 = jnp.bfloat16


def generic(parent_inverse, panel, diag_inverse, pattern, widths):
    block_size = panel.shape[2]
    half_cols = block_size // lax.axis_size("sub")
    sub_idx = lax.axis_index("sub")
    col_idx = lax.axis_index("col")
    col_mask = jnp.arange(block_size)[None, :] < widths[:, None]
    masked = panel * col_mask[:, None, :].astype(BF16)
    half_panel = lax.dynamic_slice_in_dim(masked, sub_idx * half_cols, half_cols, 2)
    full_panel = lax.all_gather(half_panel, "col", axis=1, tiled=True)
    columns = lax.all_gather(parent_inverse, "row", axis=0, tiled=True)
    pat_blocks = pattern.shape[1]
    local_blocks = columns.shape[1] // block_size
    anc_count = columns.shape[0] // block_size
    blocks_all = columns.reshape(anc_count, block_size, columns.shape[1])
    owned_ids = col_idx * local_blocks + jnp.arange(local_blocks, dtype=jnp.int32)

    def one_child(child_items):
        chosen, slab_cols = child_items
        sel_rows = jnp.take(blocks_all, chosen, axis=0).reshape(pat_blocks * block_size, columns.shape[1])
        onehot = (owned_ids[:, None] == chosen[None, :]).astype(BF16)
        slab = slab_cols.reshape(pat_blocks, block_size, half_cols)
        placed = jnp.einsum("km,mbc->kbc", onehot, slab, preferred_element_type=F32)
        placed = placed.astype(BF16).reshape(local_blocks * block_size, half_cols)
        return jnp.dot(sel_rows, placed, preferred_element_type=F32)

    partial_value = lax.map(one_child, (pattern, full_panel))
    summed = lax.psum_scatter(partial_value, "col", scatter_dimension=1, tiled=True)
    off_block = (-summed).astype(BF16)
    diag_terms = jnp.einsum("jrb,jrc->jbc", masked, off_block, preferred_element_type=F32)
    diag_total = lax.psum(diag_terms, "col")
    mask_half = lax.dynamic_slice_in_dim(col_mask, sub_idx * half_cols, half_cols, 1)
    diag_mask = (col_mask[:, :, None] & mask_half[:, None, :]).astype(F32)
    diag_block = (diag_inverse.astype(F32) * diag_mask - diag_total).astype(BF16)
    return (off_block, diag_block)


def places(ids, pat, blocks, width, children, chunks):
    c = ids[1]
    per_col = blocks // 2
    for j in range(children):
        for q in range(2 * chunks):
            g = (c if q < chunks else 1 - c) * chunks + q % chunks
            anc = pat[j, g // 2]
            side = jnp.where(anc // per_col == c, 0, per_col)
            start = (side + anc % per_col) * width + (g % 2) * 128
            yield j, q, pl.ds(pl.multiple_of(start, 128), 128)


def spread_kernel(ids, pat, panel, same, out):
    children, rows, width = panel.shape
    lane = width // 2
    chunks = rows // 128
    low = pl.ds(pl.multiple_of(ids[2] * lane, 128), lane)
    out[...] = jnp.zeros_like(out)
    for j, q, here in places(ids, pat, out.shape[0] // width, width, children, chunks):
        mine = slice(j * lane, (j + 1) * lane)
        band = slice(q % chunks * 128, (q % chunks + 1) * 128)
        if q < chunks:
            out[here, mine] = panel[j, band, low]
        else:
            out[here, mine] = same[j, band, :]


def widen_kernel(ids, pat, panel, same, *refs):
    *cross, out = refs
    children, rows, width = panel.shape
    lane = width // 2
    s = ids[2]
    chunks = rows // 128
    out[...] = jnp.zeros_like(out)
    for j, q, here in places(ids, pat, out.shape[0] // width, width, children, chunks):
        band = slice(q % chunks * 128, (q % chunks + 1) * 128)
        if q < chunks:
            out[here, j * width : (j + 1) * width] = panel[j, band, :]
        else:
            part, at = divmod(j, cross[0].shape[0])
            out[here, pl.ds(pl.multiple_of(j * width + s * lane, 128), lane)] = same[j, band, :]
            out[here, pl.ds(pl.multiple_of(j * width + (1 - s) * lane, 128), lane)] = cross[part][at, band, :]


def pick(s, first, second):
    return jnp.where(s == 0, first[...], second[...])


def product(rows, spread):
    return jnp.dot(rows, spread, preferred_element_type=F32)


def stage_kernel(a, b, a_out, b_out):
    a_out[...] = a[...]
    b_out[...] = b[...]


def early_kernel(ids, parent, z1, z1_sib, z2, z2_sib, spread, y0, acc):
    s = ids[2]
    tall, wide = parent.shape
    low, high = spread[:wide, :], spread[wide:, :]
    y0[...] = (-(product(parent[...], low) + product(pick(s, z2_sib, z2), high))).astype(BF16)
    for k, first, second in ((1, z1_sib, z1), (2, z2, z2_sib), (3, z1, z1_sib)):
        acc[(k - 1) * tall : k * tall, :] = product(pick(s, first, second), low)


def final_kernel(
    ids, pat, widths, q1, q1_sib, q2, q2_sib, spread, full, y0, acc, dinv, off_out, diag_out, y_all
):
    r, c, s = ids[0], ids[1], ids[2]
    children, width, lane = dinv.shape
    tall, wide = q1.shape
    total = y_all.shape[0]
    high = spread[wide:, :]

    def place(k, y, first=0):
        at = lax.rem(jnp.bitwise_xor(r, k) * tall + c * wide, total) + first
        y_all[pl.ds(pl.multiple_of(at, 64), y.shape[0]), :] = y

    place(0, y0[...])
    cut = q2.shape[0]
    for k, first, second, begin in ((3, q2_sib, q2, 0), (3, q2, q2_sib, cut), (1, q1_sib, q1, 0), (2, q1, q1_sib, 0)):
        at = (k - 1) * tall + begin
        rows = pick(s, first, second)
        place(k, (-(acc[at : at + rows.shape[0], :] + product(rows, high))).astype(BF16), begin)
    chunks = off_out.shape[1] // 128
    for j in range(children):
        w = widths[j]
        mine = slice(j * lane, (j + 1) * lane)
        keep_b = s * lane + lax.broadcasted_iota(jnp.int32, (1, lane), 1) < w
        keep_a = lax.broadcasted_iota(jnp.int32, (width, 1), 0) < w
        for q in range(chunks):
            g = c * chunks + q
            start = lax.rem(pat[j, g // 2] * width + (g % 2) * 128 + c * wide, total)
            got = y_all[pl.ds(pl.multiple_of(start, 128), 128), mine]
            off_out[j, q * 128 : (q + 1) * 128, :] = jnp.where(keep_b, got, jnp.zeros_like(got))
        terms = lax.dot_general(
            y_all[:, mine], full[:, j * width : (j + 1) * width], (((0,), (0,)), ((), ())), preferred_element_type=F32
        )
        diag = dinv[j].astype(F32) - terms.T
        diag_out[j] = jnp.where(keep_a & keep_b, diag, 0.0).astype(BF16)


VMEM = pl.BlockSpec(memory_space=pltpu.VMEM)
SMEM = pl.BlockSpec(memory_space=pltpu.SMEM)


def cost(flops):
    return pl.CostEstimate(flops=flops, bytes_accessed=0, transcendentals=0)


FREE = cost(0)


def gathered(parent, panel, diag_inverse, pattern, widths):
    r, c, s = lax.axis_index("row"), lax.axis_index("col"), lax.axis_index("sub")
    children, rows, width = panel.shape
    lane = width // 2
    tall, wide = parent.shape
    lanes = children * lane
    ids = jnp.stack([r, c, s]).astype(jnp.int32)

    def core(first, second):
        pairs = []
        for row in range(4):
            for col in range(2):
                for sub, to in enumerate((first, second)):
                    if to is not None:
                        to_row, to_col = to(row, col)
                        pairs.append(((row * 2 + col) * 2 + sub, (to_row * 2 + to_col) * 2 + sub))
        return pairs

    def along(d):
        return lambda row, col: (row ^ d, col)

    def across(row, col):
        return row, 1 - col

    def send(x, first, second):
        return lax.ppermute(x, ("row", "col", "sub"), core(first, second))

    def sib(x):
        return lax.ppermute(x, "sub", SWAP)

    def params(mib):
        return pltpu.CompilerParams(vmem_limit_bytes=mib << 20)

    z1 = send(parent, along(3), along(1))
    z2 = send(parent, along(2), across)
    mine = lax.dynamic_slice_in_dim(panel, s * lane, lane, 2)
    same = lax.ppermute(mine, "col", SWAP)
    q1 = send(z2, across, along(1))
    cut = tall // 2
    q2 = send(jnp.where(s == 0, z1[cut:], z2[:cut]), across, along(3))
    cross = [sib(same[: children // 2]), sib(same[children // 2 :])]

    spread = pl.pallas_call(
        spread_kernel,
        out_shape=jax.ShapeDtypeStruct((2 * wide, lanes), BF16),
        in_specs=[SMEM, SMEM] + [VMEM] * 2,
        out_specs=VMEM,
        cost_estimate=cost(500000000),
        compiler_params=params(8),
        name="spread",
    )(ids, pattern, panel, same)
    full = pl.pallas_call(
        widen_kernel,
        out_shape=jax.ShapeDtypeStruct((2 * wide, 2 * lanes), BF16),
        in_specs=[SMEM, SMEM] + [VMEM] * 4,
        out_specs=VMEM,
        cost_estimate=FREE,
        compiler_params=params(8),
        name="widen",
    )(ids, pattern, panel, same, *cross)
    z1_sib, z2_sib = sib(z1), sib(z2)
    z1_near, z2_sib = pl.pallas_call(
        stage_kernel,
        out_shape=(jax.ShapeDtypeStruct(z1.shape, BF16),) * 2,
        in_specs=[VMEM] * 2,
        out_specs=(VMEM, VMEM),
        cost_estimate=FREE,
        compiler_params=params(8),
        name="stage",
    )(z1, z2_sib)
    q1, z1_near, z2_sib = lax.optimization_barrier((q1, z1_near, z2_sib))
    y0, acc = pl.pallas_call(
        early_kernel,
        out_shape=(
            jax.ShapeDtypeStruct((tall, lanes), BF16),
            jax.ShapeDtypeStruct((3 * tall, lanes), F32),
        ),
        in_specs=[SMEM] + [VMEM] * 6,
        out_specs=(VMEM, VMEM),
        cost_estimate=cost(800000000),
        compiler_params=params(12),
        name="early",
    )(ids, parent, z1_near, z1_sib, z2, z2_sib, spread)
    q2, y0, acc = lax.optimization_barrier((q2, y0, acc))
    return pl.pallas_call(
        final_kernel,
        out_shape=(
            jax.ShapeDtypeStruct((children, rows, lane), BF16),
            jax.ShapeDtypeStruct((children, width, lane), BF16),
        ),
        in_specs=[SMEM, SMEM, SMEM] + [VMEM] * 9,
        out_specs=(VMEM, VMEM),
        scratch_shapes=[pltpu.VMEM((4 * tall, lanes), BF16)],
        cost_estimate=FREE,
        compiler_params=params(16),
        name="final",
    )(ids, pattern, widths, q1, sib(q1), q2, sib(q2), spread, full, y0, acc, diag_inverse)


def solution(mesh):
    placed = (
        P(("pole", "row"), "col"),
        P(("pole", "row"), "col", None),
        P(("pole", "row"), None, "sub"),
        P("row", None),
        P("row"),
    )
    shape = dict(mesh.shape)
    fits = (shape["row"], shape["col"], shape["sub"]) == (4, 2, 2)
    return jax.shard_map(
        gathered if fits else generic,
        mesh=mesh,
        in_specs=placed,
        out_specs=(P(("pole", "row"), "col", "sub"), P(("pole", "row"), None, "sub")),
        check_vma=False,
    )
```

```python
import jax
import jax.numpy as jnp
from jax import lax
from jax.experimental import pallas as pl
from jax.experimental.pallas import tpu as pltpu
from jax.sharding import PartitionSpec as P

SWAP = [(0, 1), (1, 0)]
F32 = jnp.float32
BF16 = jnp.bfloat16


def generic(parent_inverse, panel, diag_inverse, pattern, widths):
    block_size = panel.shape[2]
    half_cols = block_size // lax.axis_size("sub")
    sub_idx = lax.axis_index("sub")
    col_idx = lax.axis_index("col")
    col_mask = jnp.arange(block_size)[None, :] < widths[:, None]
    masked = panel * col_mask[:, None, :].astype(BF16)
    half_panel = lax.dynamic_slice_in_dim(masked, sub_idx * half_cols, half_cols, 2)
    full_panel = lax.all_gather(half_panel, "col", axis=1, tiled=True)
    columns = lax.all_gather(parent_inverse, "row", axis=0, tiled=True)
    pat_blocks = pattern.shape[1]
    local_blocks = columns.shape[1] // block_size
    anc_count = columns.shape[0] // block_size
    blocks_all = columns.reshape(anc_count, block_size, columns.shape[1])
    owned_ids = col_idx * local_blocks + jnp.arange(local_blocks, dtype=jnp.int32)

    def one_child(child_items):
        chosen, slab_cols = child_items
        sel_rows = jnp.take(blocks_all, chosen, axis=0).reshape(pat_blocks * block_size, columns.shape[1])
        onehot = (owned_ids[:, None] == chosen[None, :]).astype(BF16)
        slab = slab_cols.reshape(pat_blocks, block_size, half_cols)
        placed = jnp.einsum("km,mbc->kbc", onehot, slab, preferred_element_type=F32)
        placed = placed.astype(BF16).reshape(local_blocks * block_size, half_cols)
        return jnp.dot(sel_rows, placed, preferred_element_type=F32)

    partial_value = lax.map(one_child, (pattern, full_panel))
    summed = lax.psum_scatter(partial_value, "col", scatter_dimension=1, tiled=True)
    off_block = (-summed).astype(BF16)
    diag_terms = jnp.einsum("jrb,jrc->jbc", masked, off_block, preferred_element_type=F32)
    diag_total = lax.psum(diag_terms, "col")
    mask_half = lax.dynamic_slice_in_dim(col_mask, sub_idx * half_cols, half_cols, 1)
    diag_mask = (col_mask[:, :, None] & mask_half[:, None, :]).astype(F32)
    diag_block = (diag_inverse.astype(F32) * diag_mask - diag_total).astype(BF16)
    return (off_block, diag_block)


def places(ids, pat, blocks, width, children, chunks):
    c = ids[1]
    per_col = blocks // 2
    for j in range(children):
        for q in range(2 * chunks):
            g = (c if q < chunks else 1 - c) * chunks + q % chunks
            anc = pat[j, g // 2]
            side = jnp.where(anc // per_col == c, 0, per_col)
            start = (side + anc % per_col) * width + (g % 2) * 128
            yield j, q, pl.ds(pl.multiple_of(start, 128), 128)


def spread_kernel(ids, pat, panel, same, out):
    children, rows, width = panel.shape
    lane = width // 2
    chunks = rows // 128
    low = pl.ds(pl.multiple_of(ids[2] * lane, 128), lane)
    out[...] = jnp.zeros_like(out)
    for j, q, here in places(ids, pat, out.shape[0] // width, width, children, chunks):
        mine = slice(j * lane, (j + 1) * lane)
        band = slice(q % chunks * 128, (q % chunks + 1) * 128)
        if q < chunks:
            out[here, mine] = panel[j, band, low]
        else:
            out[here, mine] = same[j, band, :]


def widen_kernel(ids, pat, panel, same, *refs):
    *cross, out = refs
    children, rows, width = panel.shape
    lane = width // 2
    s = ids[2]
    chunks = rows // 128
    out[...] = jnp.zeros_like(out)
    for j, q, here in places(ids, pat, out.shape[0] // width, width, children, chunks):
        band = slice(q % chunks * 128, (q % chunks + 1) * 128)
        if q < chunks:
            out[here, j * width : (j + 1) * width] = panel[j, band, :]
        else:
            part, at = divmod(j, cross[0].shape[0])
            out[here, pl.ds(pl.multiple_of(j * width + s * lane, 128), lane)] = same[j, band, :]
            out[here, pl.ds(pl.multiple_of(j * width + (1 - s) * lane, 128), lane)] = cross[part][at, band, :]


def pick(s, first, second):
    return jnp.where(s == 0, first[...], second[...])


def product(rows, spread):
    return jnp.dot(rows, spread, preferred_element_type=F32)


def stage_kernel(src, out):
    out[...] = src[...]


def early_kernel(ids, parent, z2, z2_sib, spread, y0, acc2):
    s = ids[2]
    wide = parent.shape[1]
    low, high = spread[:wide, :], spread[wide:, :]
    y0[...] = (-(product(parent[...], low) + product(pick(s, z2_sib, z2), high))).astype(BF16)
    acc2[...] = product(pick(s, z2, z2_sib), low)


def middle_kernel(ids, z1, z1_sib, spread, acc13):
    s = ids[2]
    tall, wide = z1.shape
    low = spread[:wide, :]
    acc13[:tall, :] = product(pick(s, z1_sib, z1), low)
    acc13[tall:, :] = product(pick(s, z1, z1_sib), low)


def final_kernel(
    ids, pat, widths, q1, q1_sib, q2, q2_sib, spread, full, y0, acc2, acc13, dinv, off_out, diag_out, y_all
):
    r, c, s = ids[0], ids[1], ids[2]
    children, width, lane = dinv.shape
    tall, wide = q1.shape
    total = y_all.shape[0]
    high = spread[wide:, :]

    def place(k, y, first=0):
        at = lax.rem(jnp.bitwise_xor(r, k) * tall + c * wide, total) + first
        y_all[pl.ds(pl.multiple_of(at, 64), y.shape[0]), :] = y

    place(0, y0[...])
    cut = q2.shape[0]
    for k, first, second, acc, begin in (
        (3, q2_sib, q2, acc13.at[tall : tall + cut, :], 0),
        (3, q2, q2_sib, acc13.at[tall + cut :, :], cut),
        (1, q1_sib, q1, acc13.at[:tall, :], 0),
        (2, q1, q1_sib, acc2, 0),
    ):
        place(k, (-(acc[...] + product(pick(s, first, second), high))).astype(BF16), begin)
    chunks = off_out.shape[1] // 128
    for j in range(children):
        w = widths[j]
        mine = slice(j * lane, (j + 1) * lane)
        keep_b = s * lane + lax.broadcasted_iota(jnp.int32, (1, lane), 1) < w
        keep_a = lax.broadcasted_iota(jnp.int32, (width, 1), 0) < w
        for q in range(chunks):
            g = c * chunks + q
            start = lax.rem(pat[j, g // 2] * width + (g % 2) * 128 + c * wide, total)
            got = y_all[pl.ds(pl.multiple_of(start, 128), 128), mine]
            off_out[j, q * 128 : (q + 1) * 128, :] = jnp.where(keep_b, got, jnp.zeros_like(got))
        terms = lax.dot_general(
            y_all[:, mine], full[:, j * width : (j + 1) * width], (((0,), (0,)), ((), ())), preferred_element_type=F32
        )
        diag = dinv[j].astype(F32) - terms.T
        diag_out[j] = jnp.where(keep_a & keep_b, diag, 0.0).astype(BF16)


VMEM = pl.BlockSpec(memory_space=pltpu.VMEM)
SMEM = pl.BlockSpec(memory_space=pltpu.SMEM)


def cost(flops):
    return pl.CostEstimate(flops=flops, bytes_accessed=0, transcendentals=0)


FREE = cost(0)


def gathered(parent, panel, diag_inverse, pattern, widths):
    r, c, s = lax.axis_index("row"), lax.axis_index("col"), lax.axis_index("sub")
    children, rows, width = panel.shape
    lane = width // 2
    tall, wide = parent.shape
    lanes = children * lane
    ids = jnp.stack([r, c, s]).astype(jnp.int32)

    def core(first, second):
        pairs = []
        for row in range(4):
            for col in range(2):
                for sub, to in enumerate((first, second)):
                    if to is not None:
                        to_row, to_col = to(row, col)
                        pairs.append(((row * 2 + col) * 2 + sub, (to_row * 2 + to_col) * 2 + sub))
        return pairs

    def along(d):
        return lambda row, col: (row ^ d, col)

    def across(row, col):
        return row, 1 - col

    def send(x, first, second):
        return lax.ppermute(x, ("row", "col", "sub"), core(first, second))

    def sib(x):
        return lax.ppermute(x, "sub", SWAP)

    def params(mib):
        return pltpu.CompilerParams(vmem_limit_bytes=mib << 20)

    z1 = send(parent, along(3), along(1))
    z2 = send(parent, along(2), across)
    mine = lax.dynamic_slice_in_dim(panel, s * lane, lane, 2)
    same = lax.ppermute(mine, "col", SWAP)
    q1 = send(z2, across, along(1))
    cut = tall // 2
    q2 = send(jnp.where(s == 0, z1[cut:], z2[:cut]), across, along(3))
    cross = [sib(same[: children // 2]), sib(same[children // 2 :])]

    spread = pl.pallas_call(
        spread_kernel,
        out_shape=jax.ShapeDtypeStruct((2 * wide, lanes), BF16),
        in_specs=[SMEM, SMEM] + [VMEM] * 2,
        out_specs=VMEM,
        cost_estimate=cost(300000000),
        compiler_params=params(8),
        name="spread",
    )(ids, pattern, panel, same)
    full = pl.pallas_call(
        widen_kernel,
        out_shape=jax.ShapeDtypeStruct((2 * wide, 2 * lanes), BF16),
        in_specs=[SMEM, SMEM] + [VMEM] * 4,
        out_specs=VMEM,
        cost_estimate=FREE,
        compiler_params=params(8),
        name="widen",
    )(ids, pattern, panel, same, *cross)
    y_shape = jax.ShapeDtypeStruct((tall, lanes), BF16)
    z1_near = pl.pallas_call(
        stage_kernel,
        out_shape=jax.ShapeDtypeStruct(z1.shape, BF16),
        in_specs=[VMEM],
        out_specs=VMEM,
        cost_estimate=FREE,
        compiler_params=params(8),
        name="stage",
    )(z1)
    y0, acc2 = pl.pallas_call(
        early_kernel,
        out_shape=(y_shape, jax.ShapeDtypeStruct((tall, lanes), F32)),
        in_specs=[SMEM] + [VMEM] * 4,
        out_specs=(VMEM, VMEM),
        cost_estimate=cost(300000000),
        compiler_params=params(12),
        name="early",
    )(ids, parent, z2, sib(z2), spread)
    acc13 = pl.pallas_call(
        middle_kernel,
        out_shape=jax.ShapeDtypeStruct((2 * tall, lanes), F32),
        in_specs=[SMEM] + [VMEM] * 3,
        out_specs=VMEM,
        cost_estimate=FREE,
        compiler_params=params(12),
        name="middle",
    )(ids, z1_near, sib(z1), spread)
    q1, *_ = lax.optimization_barrier((q1, z1_near, spread, y0, acc2))
    q2, *_ = lax.optimization_barrier((q2, acc13))
    return pl.pallas_call(
        final_kernel,
        out_shape=(
            jax.ShapeDtypeStruct((children, rows, lane), BF16),
            jax.ShapeDtypeStruct((children, width, lane), BF16),
        ),
        in_specs=[SMEM, SMEM, SMEM] + [VMEM] * 10,
        out_specs=(VMEM, VMEM),
        scratch_shapes=[pltpu.VMEM((4 * tall, lanes), BF16)],
        cost_estimate=FREE,
        compiler_params=params(16),
        name="final",
    )(ids, pattern, widths, q1, sib(q1), q2, sib(q2), spread, full, y0, acc2, acc13, diag_inverse)


def solution(mesh):
    placed = (
        P(("pole", "row"), "col"),
        P(("pole", "row"), "col", None),
        P(("pole", "row"), None, "sub"),
        P("row", None),
        P("row"),
    )
    shape = dict(mesh.shape)
    fits = (shape["row"], shape["col"], shape["sub"]) == (4, 2, 2)
    return jax.shard_map(
        gathered if fits else generic,
        mesh=mesh,
        in_specs=placed,
        out_specs=(P(("pole", "row"), "col", "sub"), P(("pole", "row"), None, "sub")),
        check_vma=False,
    )
```

```python
import jax
import jax.numpy as jnp
from jax import lax
from jax.experimental import pallas as pl
from jax.experimental.pallas import tpu as pltpu
from jax.sharding import PartitionSpec as P

SWAP = [(0, 1), (1, 0)]
F32 = jnp.float32
BF16 = jnp.bfloat16


def generic(parent_inverse, panel, diag_inverse, pattern, widths):
    block_size = panel.shape[2]
    half_cols = block_size // lax.axis_size("sub")
    sub_idx = lax.axis_index("sub")
    col_idx = lax.axis_index("col")
    col_mask = jnp.arange(block_size)[None, :] < widths[:, None]
    masked = panel * col_mask[:, None, :].astype(BF16)
    half_panel = lax.dynamic_slice_in_dim(masked, sub_idx * half_cols, half_cols, 2)
    full_panel = lax.all_gather(half_panel, "col", axis=1, tiled=True)
    columns = lax.all_gather(parent_inverse, "row", axis=0, tiled=True)
    pat_blocks = pattern.shape[1]
    local_blocks = columns.shape[1] // block_size
    anc_count = columns.shape[0] // block_size
    blocks_all = columns.reshape(anc_count, block_size, columns.shape[1])
    owned_ids = col_idx * local_blocks + jnp.arange(local_blocks, dtype=jnp.int32)

    def one_child(child_items):
        chosen, slab_cols = child_items
        sel_rows = jnp.take(blocks_all, chosen, axis=0).reshape(pat_blocks * block_size, columns.shape[1])
        onehot = (owned_ids[:, None] == chosen[None, :]).astype(BF16)
        slab = slab_cols.reshape(pat_blocks, block_size, half_cols)
        placed = jnp.einsum("km,mbc->kbc", onehot, slab, preferred_element_type=F32)
        placed = placed.astype(BF16).reshape(local_blocks * block_size, half_cols)
        return jnp.dot(sel_rows, placed, preferred_element_type=F32)

    partial_value = lax.map(one_child, (pattern, full_panel))
    summed = lax.psum_scatter(partial_value, "col", scatter_dimension=1, tiled=True)
    off_block = (-summed).astype(BF16)
    diag_terms = jnp.einsum("jrb,jrc->jbc", masked, off_block, preferred_element_type=F32)
    diag_total = lax.psum(diag_terms, "col")
    mask_half = lax.dynamic_slice_in_dim(col_mask, sub_idx * half_cols, half_cols, 1)
    diag_mask = (col_mask[:, :, None] & mask_half[:, None, :]).astype(F32)
    diag_block = (diag_inverse.astype(F32) * diag_mask - diag_total).astype(BF16)
    return (off_block, diag_block)


def places(ids, pat, blocks, width, children, chunks):
    c = ids[1]
    per_col = blocks // 2
    for j in range(children):
        for q in range(2 * chunks):
            g = (c if q < chunks else 1 - c) * chunks + q % chunks
            anc = pat[j, g // 2]
            side = jnp.where(anc // per_col == c, 0, per_col)
            start = (side + anc % per_col) * width + (g % 2) * 128
            yield j, q, pl.ds(pl.multiple_of(start, 128), 128)


def ready_kernel(ids, pat, panel, out, wide_out):
    children, rows, width = panel.shape
    lane = width // 2
    chunks = rows // 128
    low = pl.ds(pl.multiple_of(ids[2] * lane, 128), lane)
    out[...] = jnp.zeros_like(out)
    wide_out[...] = jnp.zeros_like(wide_out)
    for j, q, here in places(ids, pat, out.shape[0] // width, width, children, chunks):
        if q < chunks:
            band = slice(q * 128, (q + 1) * 128)
            out[here, j * lane : (j + 1) * lane] = panel[j, band, low]
            wide_out[here, j * width : (j + 1) * width] = panel[j, band, :]


def spread_kernel(ids, pat, same, ready, out):
    children, rows, lane = same.shape
    width, chunks = 2 * lane, rows // 128
    out[...] = ready[...]
    for j, q, here in places(ids, pat, out.shape[0] // width, width, children, chunks):
        if q >= chunks:
            out[here, j * lane : (j + 1) * lane] = same[j, (q - chunks) * 128 : (q - chunks + 1) * 128, :]


def widen_kernel(ids, pat, same, *refs):
    *cross, ready, out = refs
    children, rows, lane = same.shape
    width, chunks = 2 * lane, rows // 128
    s = ids[2]
    out[...] = ready[...]
    for j, q, here in places(ids, pat, out.shape[0] // width, width, children, chunks):
        if q >= chunks:
            band = slice((q - chunks) * 128, (q - chunks + 1) * 128)
            part, at = divmod(j, cross[0].shape[0])
            out[here, pl.ds(pl.multiple_of(j * width + s * lane, 128), lane)] = same[j, band, :]
            out[here, pl.ds(pl.multiple_of(j * width + (1 - s) * lane, 128), lane)] = cross[part][at, band, :]


def pick(s, first, second):
    return jnp.where(s == 0, first[...], second[...])


def product(rows, spread):
    return jnp.dot(rows, spread, preferred_element_type=F32)


def early_kernel(ids, parent, z2, z2_sib, spread, y0, acc2):
    s = ids[2]
    wide = parent.shape[1]
    low, high = spread[:wide, :], spread[wide:, :]
    y0[...] = (-(product(parent[...], low) + product(pick(s, z2_sib, z2), high))).astype(BF16)
    acc2[...] = product(pick(s, z2, z2_sib), low)


def middle_kernel(ids, z1, z1_sib, spread, acc13):
    s = ids[2]
    tall, wide = z1.shape
    low = spread[:wide, :]
    acc13[pl.ds(pl.multiple_of(s * tall, 128), tall), :] = product(z1_sib[...], low)
    acc13[pl.ds(pl.multiple_of((1 - s) * tall, 128), tall), :] = product(z1[...], low)


def final_kernel(
    ids, pat, widths, q1, q1_sib, q2, q2_sib, spread, full, y0, acc2, acc13, dinv, off_out, diag_out, y_all
):
    r, c, s = ids[0], ids[1], ids[2]
    children, width, lane = dinv.shape
    tall, wide = q1.shape
    total = y_all.shape[0]
    high = spread[wide:, :]

    def place(k, y, first=0):
        at = lax.rem(jnp.bitwise_xor(r, k) * tall + c * wide, total) + first
        y_all[pl.ds(pl.multiple_of(at, 64), y.shape[0]), :] = y

    place(0, y0[...])
    cut = q2.shape[0]
    for k, first, second, acc, begin in (
        (3, q2_sib, q2, acc13.at[tall : tall + cut, :], 0),
        (3, q2, q2_sib, acc13.at[tall + cut :, :], cut),
        (1, q1_sib, q1, acc13.at[:tall, :], 0),
        (2, q1, q1_sib, acc2, 0),
    ):
        place(k, (-(acc[...] + product(pick(s, first, second), high))).astype(BF16), begin)
    chunks = off_out.shape[1] // 128
    for j in range(children):
        w = widths[j]
        mine = slice(j * lane, (j + 1) * lane)
        keep_b = s * lane + lax.broadcasted_iota(jnp.int32, (1, lane), 1) < w
        keep_a = lax.broadcasted_iota(jnp.int32, (width, 1), 0) < w
        for q in range(chunks):
            g = c * chunks + q
            start = lax.rem(pat[j, g // 2] * width + (g % 2) * 128 + c * wide, total)
            got = y_all[pl.ds(pl.multiple_of(start, 128), 128), mine]
            off_out[j, q * 128 : (q + 1) * 128, :] = jnp.where(keep_b, got, jnp.zeros_like(got))
        terms = lax.dot_general(
            y_all[:, mine], full[:, j * width : (j + 1) * width], (((0,), (0,)), ((), ())), preferred_element_type=F32
        )
        diag = dinv[j].astype(F32) - terms.T
        diag_out[j] = jnp.where(keep_a & keep_b, diag, 0.0).astype(BF16)


VMEM = pl.BlockSpec(memory_space=pltpu.VMEM)
SMEM = pl.BlockSpec(memory_space=pltpu.SMEM)
ANY = pl.BlockSpec(memory_space=pl.ANY)


def cost(flops):
    return pl.CostEstimate(flops=flops, bytes_accessed=0, transcendentals=0)


FREE = cost(0)


def gathered(parent, panel, diag_inverse, pattern, widths):
    r, c, s = lax.axis_index("row"), lax.axis_index("col"), lax.axis_index("sub")
    children, rows, width = panel.shape
    lane = width // 2
    tall, wide = parent.shape
    lanes = children * lane
    ids = jnp.stack([r, c, s]).astype(jnp.int32)

    def core(first, second):
        pairs = []
        for row in range(4):
            for col in range(2):
                for sub, to in enumerate((first, second)):
                    if to is not None:
                        to_row, to_col = to(row, col)
                        pairs.append(((row * 2 + col) * 2 + sub, (to_row * 2 + to_col) * 2 + sub))
        return pairs

    def along(d):
        return lambda row, col: (row ^ d, col)

    def across(row, col):
        return row, 1 - col

    def send(x, first, second):
        return lax.ppermute(x, ("row", "col", "sub"), core(first, second))

    def sib(x):
        return lax.ppermute(x, "sub", SWAP)

    def params(mib):
        return pltpu.CompilerParams(vmem_limit_bytes=mib << 20)

    z1 = send(parent, along(3), along(1))
    z2 = send(parent, along(2), across)
    mine = lax.dynamic_slice_in_dim(panel, s * lane, lane, 2)
    same = lax.ppermute(mine, "col", SWAP)
    q1 = send(z2, across, along(1))
    cut = tall // 2
    q2 = send(jnp.where(s == 0, z1[cut:], z2[:cut]), across, along(3))
    cross = [sib(same[: children // 2]), sib(same[children // 2 :])]

    placed = (
        jax.ShapeDtypeStruct((2 * wide, lanes), BF16),
        jax.ShapeDtypeStruct((2 * wide, 2 * lanes), BF16),
    )
    ready, wide_ready = pl.pallas_call(
        ready_kernel,
        out_shape=placed,
        in_specs=[SMEM, SMEM, VMEM],
        out_specs=(VMEM, VMEM),
        cost_estimate=FREE,
        compiler_params=params(8),
        name="ready",
    )(ids, pattern, panel)
    spread = pl.pallas_call(
        spread_kernel,
        out_shape=placed[0],
        in_specs=[SMEM, SMEM, VMEM, VMEM],
        out_specs=VMEM,
        cost_estimate=cost(0),
        compiler_params=params(8),
        name="spread",
    )(ids, pattern, same, ready)
    full = pl.pallas_call(
        widen_kernel,
        out_shape=placed[1],
        in_specs=[SMEM, SMEM] + [VMEM] * 4,
        out_specs=VMEM,
        cost_estimate=FREE,
        compiler_params=params(8),
        name="widen",
    )(ids, pattern, same, *cross, wide_ready)
    y_shape = jax.ShapeDtypeStruct((tall, lanes), BF16)
    y0, acc2 = pl.pallas_call(
        early_kernel,
        out_shape=(y_shape, jax.ShapeDtypeStruct((tall, lanes), F32)),
        in_specs=[SMEM] + [VMEM] * 4,
        out_specs=(VMEM, VMEM),
        cost_estimate=cost(0),
        compiler_params=params(12),
        name="early",
    )(ids, parent, z2, sib(z2), spread)
    acc13 = pl.pallas_call(
        middle_kernel,
        out_shape=jax.ShapeDtypeStruct((2 * tall, lanes), F32),
        in_specs=[SMEM] + [VMEM] * 3,
        out_specs=VMEM,
        cost_estimate=FREE,
        compiler_params=params(12),
        name="middle",
    )(ids, z1, sib(z1), spread)
    q1, *_ = lax.optimization_barrier((q1, spread, y0, acc2))
    q2, *_ = lax.optimization_barrier((q2, acc13))
    return pl.pallas_call(
        final_kernel,
        out_shape=(
            jax.ShapeDtypeStruct((children, rows, lane), BF16),
            jax.ShapeDtypeStruct((children, width, lane), BF16),
        ),
        in_specs=[SMEM, SMEM, SMEM] + [VMEM] * 10,
        out_specs=(VMEM, VMEM),
        scratch_shapes=[pltpu.VMEM((4 * tall, lanes), BF16)],
        cost_estimate=FREE,
        compiler_params=params(16),
        name="final",
    )(ids, pattern, widths, q1, sib(q1), q2, sib(q2), spread, full, y0, acc2, acc13, diag_inverse)


def solution(mesh):
    placed = (
        P(("pole", "row"), "col"),
        P(("pole", "row"), "col", None),
        P(("pole", "row"), None, "sub"),
        P("row", None),
        P("row"),
    )
    shape = dict(mesh.shape)
    fits = (shape["row"], shape["col"], shape["sub"]) == (4, 2, 2)
    return jax.shard_map(
        gathered if fits else generic,
        mesh=mesh,
        in_specs=placed,
        out_specs=(P(("pole", "row"), "col", "sub"), P(("pole", "row"), None, "sub")),
        check_vma=False,
    )
```

```python
import jax
import jax.numpy as jnp
from jax import lax
from jax.experimental import pallas as pl
from jax.experimental.pallas import tpu as pltpu
from jax.sharding import PartitionSpec as P

SWAP = [(0, 1), (1, 0)]
F32 = jnp.float32
BF16 = jnp.bfloat16


def generic(parent_inverse, panel, diag_inverse, pattern, widths):
    block_size = panel.shape[2]
    half_cols = block_size // lax.axis_size("sub")
    sub_idx = lax.axis_index("sub")
    col_idx = lax.axis_index("col")
    col_mask = jnp.arange(block_size)[None, :] < widths[:, None]
    masked = panel * col_mask[:, None, :].astype(BF16)
    half_panel = lax.dynamic_slice_in_dim(masked, sub_idx * half_cols, half_cols, 2)
    full_panel = lax.all_gather(half_panel, "col", axis=1, tiled=True)
    columns = lax.all_gather(parent_inverse, "row", axis=0, tiled=True)
    pat_blocks = pattern.shape[1]
    local_blocks = columns.shape[1] // block_size
    anc_count = columns.shape[0] // block_size
    blocks_all = columns.reshape(anc_count, block_size, columns.shape[1])
    owned_ids = col_idx * local_blocks + jnp.arange(local_blocks, dtype=jnp.int32)

    def one_child(child_items):
        chosen, slab_cols = child_items
        sel_rows = jnp.take(blocks_all, chosen, axis=0).reshape(pat_blocks * block_size, columns.shape[1])
        onehot = (owned_ids[:, None] == chosen[None, :]).astype(BF16)
        slab = slab_cols.reshape(pat_blocks, block_size, half_cols)
        placed = jnp.einsum("km,mbc->kbc", onehot, slab, preferred_element_type=F32)
        placed = placed.astype(BF16).reshape(local_blocks * block_size, half_cols)
        return jnp.dot(sel_rows, placed, preferred_element_type=F32)

    partial_value = lax.map(one_child, (pattern, full_panel))
    summed = lax.psum_scatter(partial_value, "col", scatter_dimension=1, tiled=True)
    off_block = (-summed).astype(BF16)
    diag_terms = jnp.einsum("jrb,jrc->jbc", masked, off_block, preferred_element_type=F32)
    diag_total = lax.psum(diag_terms, "col")
    mask_half = lax.dynamic_slice_in_dim(col_mask, sub_idx * half_cols, half_cols, 1)
    diag_mask = (col_mask[:, :, None] & mask_half[:, None, :]).astype(F32)
    diag_block = (diag_inverse.astype(F32) * diag_mask - diag_total).astype(BF16)
    return (off_block, diag_block)


def places(ids, pat, blocks, width, children, chunks):
    c = ids[1]
    per_col = blocks // 2
    for j in range(children):
        for q in range(2 * chunks):
            g = (c if q < chunks else 1 - c) * chunks + q % chunks
            anc = pat[j, g // 2]
            side = jnp.where(anc // per_col == c, 0, per_col)
            start = (side + anc % per_col) * width + (g % 2) * 128
            yield j, q, pl.ds(pl.multiple_of(start, 128), 128)


def ready_kernel(ids, pat, panel, out, wide_out):
    children, rows, width = panel.shape
    lane = width // 2
    chunks = rows // 128
    low = pl.ds(pl.multiple_of(ids[2] * lane, 128), lane)
    out[...] = jnp.zeros_like(out)
    wide_out[...] = jnp.zeros_like(wide_out)
    for j, q, here in places(ids, pat, out.shape[0] // width, width, children, chunks):
        if q < chunks:
            band = slice(q * 128, (q + 1) * 128)
            out[here, j * lane : (j + 1) * lane] = panel[j, band, low]
            wide_out[here, j * width : (j + 1) * width] = panel[j, band, :]


def spread_kernel(ids, pat, same, ready, out):
    children, rows, lane = same.shape
    width, chunks = 2 * lane, rows // 128
    out[...] = ready[...]
    for j, q, here in places(ids, pat, out.shape[0] // width, width, children, chunks):
        if q >= chunks:
            out[here, j * lane : (j + 1) * lane] = same[j, (q - chunks) * 128 : (q - chunks + 1) * 128, :]


def widen_kernel(ids, pat, same, *refs):
    *cross, ready, out = refs
    children, rows, lane = same.shape
    width, chunks = 2 * lane, rows // 128
    s = ids[2]
    out[...] = ready[...]
    for j, q, here in places(ids, pat, out.shape[0] // width, width, children, chunks):
        if q >= chunks:
            band = slice((q - chunks) * 128, (q - chunks + 1) * 128)
            part, at = divmod(j, cross[0].shape[0])
            out[here, pl.ds(pl.multiple_of(j * width + s * lane, 128), lane)] = same[j, band, :]
            out[here, pl.ds(pl.multiple_of(j * width + (1 - s) * lane, 128), lane)] = cross[part][at, band, :]


def pick(s, first, second):
    return jnp.where(s == 0, first[...], second[...])


def product(rows, spread):
    return jnp.dot(rows, spread, preferred_element_type=F32)


def early_kernel(ids, parent, z2, z2_sib, spread, y0, acc2):
    s = ids[2]
    wide = parent.shape[1]
    low, high = spread[:wide, :], spread[wide:, :]
    y0[...] = (-(product(parent[...], low) + product(pick(s, z2_sib, z2), high))).astype(BF16)
    acc2[...] = product(pick(s, z2, z2_sib), low)


def middle_kernel(ids, z1, z1_sib, spread, tile, acc13, tile_out):
    tile_out[...] = tile[...]
    s = ids[2]
    tall, wide = z1.shape
    low = spread[:wide, :]
    acc13[pl.ds(pl.multiple_of(s * tall, 128), tall), :] = product(z1_sib[...], low)
    acc13[pl.ds(pl.multiple_of((1 - s) * tall, 128), tall), :] = product(z1[...], low)


def final_kernel(
    ids, pat, widths, q1, q1_sib, q2, q2_sib, spread, full, y0, acc2, acc13, dinv, off_out, diag_out, y_all
):
    r, c, s = ids[0], ids[1], ids[2]
    children, width, lane = dinv.shape
    tall, wide = q1.shape
    total = y_all.shape[0]
    high = spread[wide:, :]

    def place(k, y, first=0):
        at = lax.rem(jnp.bitwise_xor(r, k) * tall + c * wide, total) + first
        y_all[pl.ds(pl.multiple_of(at, 64), y.shape[0]), :] = y

    place(0, y0[...])
    cut = q2.shape[0]
    for k, first, second, acc, begin in (
        (3, q2_sib, q2, acc13.at[tall : tall + cut, :], 0),
        (3, q2, q2_sib, acc13.at[tall + cut :, :], cut),
        (1, q1_sib, q1, acc13.at[:tall, :], 0),
        (2, q1, q1_sib, acc2, 0),
    ):
        place(k, (-(acc[...] + product(pick(s, first, second), high))).astype(BF16), begin)
    chunks = off_out.shape[1] // 128
    for j in range(children):
        w = widths[j]
        mine = slice(j * lane, (j + 1) * lane)
        keep_b = s * lane + lax.broadcasted_iota(jnp.int32, (1, lane), 1) < w
        keep_a = lax.broadcasted_iota(jnp.int32, (width, 1), 0) < w
        for q in range(chunks):
            g = c * chunks + q
            start = lax.rem(pat[j, g // 2] * width + (g % 2) * 128 + c * wide, total)
            got = y_all[pl.ds(pl.multiple_of(start, 128), 128), mine]
            off_out[j, q * 128 : (q + 1) * 128, :] = jnp.where(keep_b, got, jnp.zeros_like(got))
        terms = lax.dot_general(
            y_all[:, mine], full[:, j * width : (j + 1) * width], (((0,), (0,)), ((), ())), preferred_element_type=F32
        )
        diag = dinv[j].astype(F32) - terms.T
        diag_out[j] = jnp.where(keep_a & keep_b, diag, 0.0).astype(BF16)


VMEM = pl.BlockSpec(memory_space=pltpu.VMEM)
SMEM = pl.BlockSpec(memory_space=pltpu.SMEM)
ANY = pl.BlockSpec(memory_space=pl.ANY)


def cost(flops):
    return pl.CostEstimate(flops=flops, bytes_accessed=0, transcendentals=0)


FREE = cost(0)


def gathered(parent, panel, diag_inverse, pattern, widths):
    r, c, s = lax.axis_index("row"), lax.axis_index("col"), lax.axis_index("sub")
    children, rows, width = panel.shape
    lane = width // 2
    tall, wide = parent.shape
    lanes = children * lane
    ids = jnp.stack([r, c, s]).astype(jnp.int32)

    def core(first, second):
        pairs = []
        for row in range(4):
            for col in range(2):
                for sub, to in enumerate((first, second)):
                    if to is not None:
                        to_row, to_col = to(row, col)
                        pairs.append(((row * 2 + col) * 2 + sub, (to_row * 2 + to_col) * 2 + sub))
        return pairs

    def along(d):
        return lambda row, col: (row ^ d, col)

    def across(row, col):
        return row, 1 - col

    def send(x, first, second):
        return lax.ppermute(x, ("row", "col", "sub"), core(first, second))

    def sib(x):
        return lax.ppermute(x, "sub", SWAP)

    def params(mib):
        return pltpu.CompilerParams(vmem_limit_bytes=mib << 20)

    z1 = send(parent, along(3), along(1))
    z2 = send(parent, along(2), across)
    mine = lax.dynamic_slice_in_dim(panel, s * lane, lane, 2)
    same = lax.ppermute(mine, "col", SWAP)
    q1 = send(z2, across, along(1))
    cut = tall // 2
    q2 = send(jnp.where(s == 0, z1[cut:], z2[:cut]), across, along(3))
    cross = [sib(same[: children // 2]), sib(same[children // 2 :])]

    placed = (
        jax.ShapeDtypeStruct((2 * wide, lanes), BF16),
        jax.ShapeDtypeStruct((2 * wide, 2 * lanes), BF16),
    )
    ready, wide_ready = pl.pallas_call(
        ready_kernel,
        out_shape=placed,
        in_specs=[SMEM, SMEM, VMEM],
        out_specs=(VMEM, VMEM),
        cost_estimate=FREE,
        compiler_params=params(8),
        name="ready",
    )(ids, pattern, panel)
    spread = pl.pallas_call(
        spread_kernel,
        out_shape=placed[0],
        in_specs=[SMEM, SMEM, VMEM, VMEM],
        out_specs=VMEM,
        cost_estimate=cost(0),
        compiler_params=params(8),
        name="spread",
    )(ids, pattern, same, ready)
    full = pl.pallas_call(
        widen_kernel,
        out_shape=placed[1],
        in_specs=[SMEM, SMEM] + [VMEM] * 4,
        out_specs=VMEM,
        cost_estimate=FREE,
        compiler_params=params(8),
        name="widen",
    )(ids, pattern, same, *cross, wide_ready)
    y_shape = jax.ShapeDtypeStruct((tall, lanes), BF16)
    y0, acc2 = pl.pallas_call(
        early_kernel,
        out_shape=(y_shape, jax.ShapeDtypeStruct((tall, lanes), F32)),
        in_specs=[SMEM] + [VMEM] * 4,
        out_specs=(VMEM, VMEM),
        cost_estimate=cost(0),
        compiler_params=params(12),
        name="early",
    )(ids, parent, z2, sib(z2), spread)
    q1, *_ = lax.optimization_barrier((q1, spread, y0, acc2))
    q1_sib = sib(q1)
    acc13, q1 = pl.pallas_call(
        middle_kernel,
        out_shape=(jax.ShapeDtypeStruct((2 * tall, lanes), F32), jax.ShapeDtypeStruct(q1.shape, BF16)),
        in_specs=[SMEM] + [VMEM] * 4,
        out_specs=(VMEM, VMEM),
        cost_estimate=FREE,
        compiler_params=params(12),
        name="middle",
    )(ids, z1, sib(z1), spread, q1)
    q2, *_ = lax.optimization_barrier((q2, acc13))
    return pl.pallas_call(
        final_kernel,
        out_shape=(
            jax.ShapeDtypeStruct((children, rows, lane), BF16),
            jax.ShapeDtypeStruct((children, width, lane), BF16),
        ),
        in_specs=[SMEM, SMEM, SMEM] + [VMEM] * 10,
        out_specs=(VMEM, VMEM),
        scratch_shapes=[pltpu.VMEM((4 * tall, lanes), BF16)],
        cost_estimate=FREE,
        compiler_params=params(16),
        name="final",
    )(ids, pattern, widths, q1, q1_sib, q2, sib(q2), spread, full, y0, acc2, acc13, diag_inverse)


def solution(mesh):
    placed = (
        P(("pole", "row"), "col"),
        P(("pole", "row"), "col", None),
        P(("pole", "row"), None, "sub"),
        P("row", None),
        P("row"),
    )
    shape = dict(mesh.shape)
    fits = (shape["row"], shape["col"], shape["sub"]) == (4, 2, 2)
    return jax.shard_map(
        gathered if fits else generic,
        mesh=mesh,
        in_specs=placed,
        out_specs=(P(("pole", "row"), "col", "sub"), P(("pole", "row"), None, "sub")),
        check_vma=False,
    )
```

```python
import jax
import jax.numpy as jnp
from jax import lax
from jax.experimental import pallas as pl
from jax.experimental.pallas import tpu as pltpu
from jax.sharding import PartitionSpec as P

SWAP = [(0, 1), (1, 0)]
F32 = jnp.float32
BF16 = jnp.bfloat16


def generic(parent_inverse, panel, diag_inverse, pattern, widths):
    block_size = panel.shape[2]
    half_cols = block_size // lax.axis_size("sub")
    sub_idx = lax.axis_index("sub")
    col_idx = lax.axis_index("col")
    col_mask = jnp.arange(block_size)[None, :] < widths[:, None]
    masked = panel * col_mask[:, None, :].astype(BF16)
    half_panel = lax.dynamic_slice_in_dim(masked, sub_idx * half_cols, half_cols, 2)
    full_panel = lax.all_gather(half_panel, "col", axis=1, tiled=True)
    columns = lax.all_gather(parent_inverse, "row", axis=0, tiled=True)
    pat_blocks = pattern.shape[1]
    local_blocks = columns.shape[1] // block_size
    anc_count = columns.shape[0] // block_size
    blocks_all = columns.reshape(anc_count, block_size, columns.shape[1])
    owned_ids = col_idx * local_blocks + jnp.arange(local_blocks, dtype=jnp.int32)

    def one_child(child_items):
        chosen, slab_cols = child_items
        sel_rows = jnp.take(blocks_all, chosen, axis=0).reshape(pat_blocks * block_size, columns.shape[1])
        onehot = (owned_ids[:, None] == chosen[None, :]).astype(BF16)
        slab = slab_cols.reshape(pat_blocks, block_size, half_cols)
        placed = jnp.einsum("km,mbc->kbc", onehot, slab, preferred_element_type=F32)
        placed = placed.astype(BF16).reshape(local_blocks * block_size, half_cols)
        return jnp.dot(sel_rows, placed, preferred_element_type=F32)

    partial_value = lax.map(one_child, (pattern, full_panel))
    summed = lax.psum_scatter(partial_value, "col", scatter_dimension=1, tiled=True)
    off_block = (-summed).astype(BF16)
    diag_terms = jnp.einsum("jrb,jrc->jbc", masked, off_block, preferred_element_type=F32)
    diag_total = lax.psum(diag_terms, "col")
    mask_half = lax.dynamic_slice_in_dim(col_mask, sub_idx * half_cols, half_cols, 1)
    diag_mask = (col_mask[:, :, None] & mask_half[:, None, :]).astype(F32)
    diag_block = (diag_inverse.astype(F32) * diag_mask - diag_total).astype(BF16)
    return (off_block, diag_block)


def places(ids, pat, blocks, width, children, chunks):
    c = ids[1]
    per_col = blocks // 2
    for j in range(children):
        for q in range(2 * chunks):
            g = (c if q < chunks else 1 - c) * chunks + q % chunks
            anc = pat[j, g // 2]
            side = jnp.where(anc // per_col == c, 0, per_col)
            start = (side + anc % per_col) * width + (g % 2) * 128
            yield j, q, pl.ds(pl.multiple_of(start, 128), 128)


def ready_kernel(ids, pat, panel, out, wide_out):
    children, rows, width = panel.shape
    lane = width // 2
    chunks = rows // 128
    low = pl.ds(pl.multiple_of(ids[2] * lane, 128), lane)
    out[...] = jnp.zeros_like(out)
    wide_out[...] = jnp.zeros_like(wide_out)
    for j, q, here in places(ids, pat, out.shape[0] // width, width, children, chunks):
        if q < chunks:
            band = slice(q * 128, (q + 1) * 128)
            out[here, j * lane : (j + 1) * lane] = panel[j, band, low]
            wide_out[here, j * width : (j + 1) * width] = panel[j, band, :]


def spread_kernel(ids, pat, same, ready, out):
    children, rows, lane = same.shape
    width, chunks = 2 * lane, rows // 128
    out[...] = ready[...]
    for j, q, here in places(ids, pat, out.shape[0] // width, width, children, chunks):
        if q >= chunks:
            out[here, j * lane : (j + 1) * lane] = same[j, (q - chunks) * 128 : (q - chunks + 1) * 128, :]


def widen_kernel(ids, pat, same, *refs):
    *cross, ready, out = refs
    children, rows, lane = same.shape
    width, chunks = 2 * lane, rows // 128
    s = ids[2]
    out[...] = ready[...]
    for j, q, here in places(ids, pat, out.shape[0] // width, width, children, chunks):
        if q >= chunks:
            band = slice((q - chunks) * 128, (q - chunks + 1) * 128)
            part, at = divmod(j, cross[0].shape[0])
            out[here, pl.ds(pl.multiple_of(j * width + s * lane, 128), lane)] = same[j, band, :]
            out[here, pl.ds(pl.multiple_of(j * width + (1 - s) * lane, 128), lane)] = cross[part][at, band, :]


def pick(s, first, second):
    return jnp.where(s == 0, first[...], second[...])


def product(rows, spread):
    return jnp.dot(rows, spread, preferred_element_type=F32)


def early_kernel(ids, pat, same, ready, parent, z1, z2, z2_sib, spread, y0, acc2, acc_own):
    s = ids[2]
    wide = parent.shape[1]
    spread_kernel(ids, pat, same, ready, spread)
    low, high = spread[:wide, :], spread[wide:, :]
    y0[...] = (-(product(parent[...], low) + product(pick(s, z2_sib, z2), high))).astype(BF16)
    acc2[...] = product(pick(s, z2, z2_sib), low)
    acc_own[...] = product(z1[...], low)


def middle_kernel(ids, acc_own, z1_sib, spread, tile, acc13, tile_out):
    s = ids[2]
    tall, wide = z1_sib.shape
    tile_out[...] = tile[...]
    acc13[pl.ds(pl.multiple_of(s * tall, 128), tall), :] = product(z1_sib[...], spread[:wide, :])
    acc13[pl.ds(pl.multiple_of((1 - s) * tall, 128), tall), :] = acc_own[...]


def final_kernel(
    ids, pat, widths, q1, q1_sib, q2, q2_sib, spread, full, y0, acc2, acc13, dinv, off_out, diag_out, y_all
):
    r, c, s = ids[0], ids[1], ids[2]
    children, width, lane = dinv.shape
    tall, wide = q1.shape
    total = y_all.shape[0]
    high = spread[wide:, :]

    def place(k, y, first=0):
        at = lax.rem(jnp.bitwise_xor(r, k) * tall + c * wide, total) + first
        y_all[pl.ds(pl.multiple_of(at, 64), y.shape[0]), :] = y

    place(0, y0[...])
    cut = q2.shape[0]
    for k, first, second, acc, begin in (
        (3, q2_sib, q2, acc13.at[tall : tall + cut, :], 0),
        (3, q2, q2_sib, acc13.at[tall + cut :, :], cut),
        (1, q1_sib, q1, acc13.at[:tall, :], 0),
        (2, q1, q1_sib, acc2, 0),
    ):
        place(k, (-(acc[...] + product(pick(s, first, second), high))).astype(BF16), begin)
    chunks = off_out.shape[1] // 128
    for j in range(children):
        w = widths[j]
        mine = slice(j * lane, (j + 1) * lane)
        keep_b = s * lane + lax.broadcasted_iota(jnp.int32, (1, lane), 1) < w
        keep_a = lax.broadcasted_iota(jnp.int32, (width, 1), 0) < w
        for q in range(chunks):
            g = c * chunks + q
            start = lax.rem(pat[j, g // 2] * width + (g % 2) * 128 + c * wide, total)
            got = y_all[pl.ds(pl.multiple_of(start, 128), 128), mine]
            off_out[j, q * 128 : (q + 1) * 128, :] = jnp.where(keep_b, got, jnp.zeros_like(got))
        terms = lax.dot_general(
            y_all[:, mine], full[:, j * width : (j + 1) * width], (((0,), (0,)), ((), ())), preferred_element_type=F32
        )
        diag = dinv[j].astype(F32) - terms.T
        diag_out[j] = jnp.where(keep_a & keep_b, diag, 0.0).astype(BF16)


VMEM = pl.BlockSpec(memory_space=pltpu.VMEM)
SMEM = pl.BlockSpec(memory_space=pltpu.SMEM)
ANY = pl.BlockSpec(memory_space=pl.ANY)


def cost(flops):
    return pl.CostEstimate(flops=flops, bytes_accessed=0, transcendentals=0)


FREE = cost(0)


def gathered(parent, panel, diag_inverse, pattern, widths):
    r, c, s = lax.axis_index("row"), lax.axis_index("col"), lax.axis_index("sub")
    children, rows, width = panel.shape
    lane = width // 2
    tall, wide = parent.shape
    lanes = children * lane
    ids = jnp.stack([r, c, s]).astype(jnp.int32)

    def core(first, second):
        pairs = []
        for row in range(4):
            for col in range(2):
                for sub, to in enumerate((first, second)):
                    if to is not None:
                        to_row, to_col = to(row, col)
                        pairs.append(((row * 2 + col) * 2 + sub, (to_row * 2 + to_col) * 2 + sub))
        return pairs

    def along(d):
        return lambda row, col: (row ^ d, col)

    def across(row, col):
        return row, 1 - col

    def send(x, first, second):
        return lax.ppermute(x, ("row", "col", "sub"), core(first, second))

    def sib(x):
        return lax.ppermute(x, "sub", SWAP)

    def params(mib):
        return pltpu.CompilerParams(vmem_limit_bytes=mib << 20)

    z1 = send(parent, along(3), along(1))
    z2 = send(parent, along(2), across)
    mine = lax.dynamic_slice_in_dim(panel, s * lane, lane, 2)
    same = lax.ppermute(mine, "col", SWAP)
    q1 = send(z2, across, along(1))
    cut = tall // 2
    q2 = send(jnp.where(s == 0, z1[cut:], z2[:cut]), across, along(3))
    cross = [sib(same[: children // 2]), sib(same[children // 2 :])]

    placed = (
        jax.ShapeDtypeStruct((2 * wide, lanes), BF16),
        jax.ShapeDtypeStruct((2 * wide, 2 * lanes), BF16),
    )
    ready, wide_ready = pl.pallas_call(
        ready_kernel,
        out_shape=placed,
        in_specs=[SMEM, SMEM, VMEM],
        out_specs=(VMEM, VMEM),
        cost_estimate=FREE,
        compiler_params=params(8),
        name="ready",
    )(ids, pattern, panel)
    full = pl.pallas_call(
        widen_kernel,
        out_shape=placed[1],
        in_specs=[SMEM, SMEM] + [VMEM] * 4,
        out_specs=VMEM,
        cost_estimate=FREE,
        compiler_params=params(8),
        name="widen",
    )(ids, pattern, same, *cross, wide_ready)
    y_shape = jax.ShapeDtypeStruct((tall, lanes), BF16)
    acc_shape = jax.ShapeDtypeStruct((tall, lanes), F32)
    spread, y0, acc2, acc_own = pl.pallas_call(
        early_kernel,
        out_shape=(placed[0], y_shape, acc_shape, acc_shape),
        in_specs=[SMEM, SMEM] + [VMEM] * 6,
        out_specs=(VMEM,) * 4,
        cost_estimate=cost(0),
        compiler_params=params(12),
        name="early",
    )(ids, pattern, same, ready, parent, z1, z2, sib(z2))
    q1, *_ = lax.optimization_barrier((q1, spread, y0, acc2, acc_own))
    q1_sib = sib(q1)
    acc13, q1 = pl.pallas_call(
        middle_kernel,
        out_shape=(jax.ShapeDtypeStruct((2 * tall, lanes), F32), jax.ShapeDtypeStruct(q1.shape, BF16)),
        in_specs=[SMEM] + [VMEM] * 4,
        out_specs=(VMEM, VMEM),
        cost_estimate=FREE,
        compiler_params=params(12),
        name="middle",
    )(ids, acc_own, sib(z1), spread, q1)
    q2, *_ = lax.optimization_barrier((q2, acc13))
    return pl.pallas_call(
        final_kernel,
        out_shape=(
            jax.ShapeDtypeStruct((children, rows, lane), BF16),
            jax.ShapeDtypeStruct((children, width, lane), BF16),
        ),
        in_specs=[SMEM, SMEM, SMEM] + [VMEM] * 10,
        out_specs=(VMEM, VMEM),
        scratch_shapes=[pltpu.VMEM((4 * tall, lanes), BF16)],
        cost_estimate=FREE,
        compiler_params=params(16),
        name="final",
    )(ids, pattern, widths, q1, q1_sib, q2, sib(q2), spread, full, y0, acc2, acc13, diag_inverse)


def solution(mesh):
    placed = (
        P(("pole", "row"), "col"),
        P(("pole", "row"), "col", None),
        P(("pole", "row"), None, "sub"),
        P("row", None),
        P("row"),
    )
    shape = dict(mesh.shape)
    fits = (shape["row"], shape["col"], shape["sub"]) == (4, 2, 2)
    return jax.shard_map(
        gathered if fits else generic,
        mesh=mesh,
        in_specs=placed,
        out_specs=(P(("pole", "row"), "col", "sub"), P(("pole", "row"), None, "sub")),
        check_vma=False,
    )
```

```python
import jax
import jax.numpy as jnp
from jax import lax
from jax.experimental import pallas as pl
from jax.experimental.pallas import tpu as pltpu
from jax.sharding import PartitionSpec as P

SWAP = [(0, 1), (1, 0)]
F32 = jnp.float32
BF16 = jnp.bfloat16


def generic(parent_inverse, panel, diag_inverse, pattern, widths):
    block_size = panel.shape[2]
    half_cols = block_size // lax.axis_size("sub")
    sub_idx = lax.axis_index("sub")
    col_idx = lax.axis_index("col")
    col_mask = jnp.arange(block_size)[None, :] < widths[:, None]
    masked = panel * col_mask[:, None, :].astype(BF16)
    half_panel = lax.dynamic_slice_in_dim(masked, sub_idx * half_cols, half_cols, 2)
    full_panel = lax.all_gather(half_panel, "col", axis=1, tiled=True)
    columns = lax.all_gather(parent_inverse, "row", axis=0, tiled=True)
    pat_blocks = pattern.shape[1]
    local_blocks = columns.shape[1] // block_size
    anc_count = columns.shape[0] // block_size
    blocks_all = columns.reshape(anc_count, block_size, columns.shape[1])
    owned_ids = col_idx * local_blocks + jnp.arange(local_blocks, dtype=jnp.int32)

    def one_child(child_items):
        chosen, slab_cols = child_items
        sel_rows = jnp.take(blocks_all, chosen, axis=0).reshape(pat_blocks * block_size, columns.shape[1])
        onehot = (owned_ids[:, None] == chosen[None, :]).astype(BF16)
        slab = slab_cols.reshape(pat_blocks, block_size, half_cols)
        placed = jnp.einsum("km,mbc->kbc", onehot, slab, preferred_element_type=F32)
        placed = placed.astype(BF16).reshape(local_blocks * block_size, half_cols)
        return jnp.dot(sel_rows, placed, preferred_element_type=F32)

    partial_value = lax.map(one_child, (pattern, full_panel))
    summed = lax.psum_scatter(partial_value, "col", scatter_dimension=1, tiled=True)
    off_block = (-summed).astype(BF16)
    diag_terms = jnp.einsum("jrb,jrc->jbc", masked, off_block, preferred_element_type=F32)
    diag_total = lax.psum(diag_terms, "col")
    mask_half = lax.dynamic_slice_in_dim(col_mask, sub_idx * half_cols, half_cols, 1)
    diag_mask = (col_mask[:, :, None] & mask_half[:, None, :]).astype(F32)
    diag_block = (diag_inverse.astype(F32) * diag_mask - diag_total).astype(BF16)
    return (off_block, diag_block)


def places(ids, pat, blocks, width, children, chunks):
    c = ids[1]
    per_col = blocks // 2
    for j in range(children):
        for q in range(2 * chunks):
            g = (c if q < chunks else 1 - c) * chunks + q % chunks
            anc = pat[j, g // 2]
            side = jnp.where(anc // per_col == c, 0, per_col)
            start = (side + anc % per_col) * width + (g % 2) * 128
            yield j, q, pl.ds(pl.multiple_of(start, 128), 128)


def ready_kernel(ids, pat, panel, out, wide_out):
    children, rows, width = panel.shape
    lane = width // 2
    chunks = rows // 128
    low = pl.ds(pl.multiple_of(ids[2] * lane, 128), lane)
    out[...] = jnp.zeros_like(out)
    wide_out[...] = jnp.zeros_like(wide_out)
    for j, q, here in places(ids, pat, out.shape[0] // width, width, children, chunks):
        if q < chunks:
            band = slice(q * 128, (q + 1) * 128)
            out[here, j * lane : (j + 1) * lane] = panel[j, band, low]
            wide_out[here, j * width : (j + 1) * width] = panel[j, band, :]


def spread_kernel(ids, pat, same, ready, out):
    children, rows, lane = same.shape
    width, chunks = 2 * lane, rows // 128
    out[...] = ready[...]
    for j, q, here in places(ids, pat, out.shape[0] // width, width, children, chunks):
        if q >= chunks:
            out[here, j * lane : (j + 1) * lane] = same[j, (q - chunks) * 128 : (q - chunks + 1) * 128, :]


def widen_kernel(ids, pat, same, *refs):
    *cross, ready, out = refs
    children, rows, lane = same.shape
    width, chunks = 2 * lane, rows // 128
    s = ids[2]
    out[...] = ready[...]
    for j, q, here in places(ids, pat, out.shape[0] // width, width, children, chunks):
        if q >= chunks:
            band = slice((q - chunks) * 128, (q - chunks + 1) * 128)
            part, at = divmod(j, cross[0].shape[0])
            out[here, pl.ds(pl.multiple_of(j * width + s * lane, 128), lane)] = same[j, band, :]
            out[here, pl.ds(pl.multiple_of(j * width + (1 - s) * lane, 128), lane)] = cross[part][at, band, :]


def pick(s, first, second):
    return jnp.where(s == 0, first[...], second[...])


def product(rows, spread):
    return jnp.dot(rows, spread, preferred_element_type=F32)


def early_kernel(ids, pat, same, ready, parent, z1, z2, z2_sib, spread, y0, acc2, acc_own):
    s = ids[2]
    wide = parent.shape[1]
    spread_kernel(ids, pat, same, ready, spread)
    low, high = spread[:wide, :], spread[wide:, :]
    y0[...] = (-(product(parent[...], low) + product(pick(s, z2_sib, z2), high))).astype(BF16)
    acc2[...] = product(pick(s, z2, z2_sib), low)
    acc_own[...] = product(z1[...], low)


def middle_kernel(ids, acc_own, z1_sib, spread, tile, acc13, tile_out):
    s = ids[2]
    tall, wide = z1_sib.shape
    tile_out[...] = tile[...]
    acc13[pl.ds(pl.multiple_of(s * tall, 128), tall), :] = product(z1_sib[...], spread[:wide, :])
    acc13[pl.ds(pl.multiple_of((1 - s) * tall, 128), tall), :] = acc_own[...]


def final_kernel(
    ids, pat, widths, q1, q1_sib, q2, q2_sib, spread, full, y0, acc2, acc13, dinv, off_out, diag_out, y_all
):
    r, c, s = ids[0], ids[1], ids[2]
    children, width, lane = dinv.shape
    tall, wide = q1.shape
    total = y_all.shape[0]
    high = spread[wide:, :]

    def place(k, y, first=0):
        at = lax.rem(jnp.bitwise_xor(r, k) * tall + c * wide, total) + first
        y_all[pl.ds(pl.multiple_of(at, 64), y.shape[0]), :] = y

    place(0, y0[...])
    cut = q2.shape[0]
    for k, first, second, acc, begin in (
        (1, q1_sib, q1, acc13.at[:tall, :], 0),
        (2, q1, q1_sib, acc2, 0),
        (3, q2_sib, q2, acc13.at[tall : tall + cut, :], 0),
        (3, q2, q2_sib, acc13.at[tall + cut :, :], cut),
    ):
        place(k, (-(acc[...] + product(pick(s, first, second), high))).astype(BF16), begin)
    chunks = off_out.shape[1] // 128
    for j in range(children):
        w = widths[j]
        mine = slice(j * lane, (j + 1) * lane)
        keep_b = s * lane + lax.broadcasted_iota(jnp.int32, (1, lane), 1) < w
        keep_a = lax.broadcasted_iota(jnp.int32, (width, 1), 0) < w
        for q in range(chunks):
            g = c * chunks + q
            start = lax.rem(pat[j, g // 2] * width + (g % 2) * 128 + c * wide, total)
            got = y_all[pl.ds(pl.multiple_of(start, 128), 128), mine]
            off_out[j, q * 128 : (q + 1) * 128, :] = jnp.where(keep_b, got, jnp.zeros_like(got))
        terms = lax.dot_general(
            y_all[:, mine], full[:, j * width : (j + 1) * width], (((0,), (0,)), ((), ())), preferred_element_type=F32
        )
        diag = dinv[j].astype(F32) - terms.T
        diag_out[j] = jnp.where(keep_a & keep_b, diag, 0.0).astype(BF16)


VMEM = pl.BlockSpec(memory_space=pltpu.VMEM)
SMEM = pl.BlockSpec(memory_space=pltpu.SMEM)
ANY = pl.BlockSpec(memory_space=pl.ANY)


def cost(flops):
    return pl.CostEstimate(flops=flops, bytes_accessed=0, transcendentals=0)


FREE = cost(0)


def gathered(parent, panel, diag_inverse, pattern, widths):
    r, c, s = lax.axis_index("row"), lax.axis_index("col"), lax.axis_index("sub")
    children, rows, width = panel.shape
    lane = width // 2
    tall, wide = parent.shape
    lanes = children * lane
    ids = jnp.stack([r, c, s]).astype(jnp.int32)

    def core(first, second):
        pairs = []
        for row in range(4):
            for col in range(2):
                for sub, to in enumerate((first, second)):
                    if to is not None:
                        to_row, to_col = to(row, col)
                        pairs.append(((row * 2 + col) * 2 + sub, (to_row * 2 + to_col) * 2 + sub))
        return pairs

    def along(d):
        return lambda row, col: (row ^ d, col)

    def across(row, col):
        return row, 1 - col

    def send(x, first, second):
        return lax.ppermute(x, ("row", "col", "sub"), core(first, second))

    def sib(x):
        return lax.ppermute(x, "sub", SWAP)

    def params(mib):
        return pltpu.CompilerParams(vmem_limit_bytes=mib << 20)

    z1 = send(parent, along(3), along(1))
    z2 = send(parent, along(2), across)
    mine = lax.dynamic_slice_in_dim(panel, s * lane, lane, 2)
    same = lax.ppermute(mine, "col", SWAP)
    q1 = send(z2, across, along(1))
    cut = tall // 2
    q2 = send(jnp.where(s == 0, z1[cut:], z2[:cut]), across, along(3))
    cross = [sib(same[: children // 2]), sib(same[children // 2 :])]

    placed = (
        jax.ShapeDtypeStruct((2 * wide, lanes), BF16),
        jax.ShapeDtypeStruct((2 * wide, 2 * lanes), BF16),
    )
    ready, wide_ready = pl.pallas_call(
        ready_kernel,
        out_shape=placed,
        in_specs=[SMEM, SMEM, VMEM],
        out_specs=(VMEM, VMEM),
        cost_estimate=FREE,
        compiler_params=params(8),
        name="ready",
    )(ids, pattern, panel)
    full = pl.pallas_call(
        widen_kernel,
        out_shape=placed[1],
        in_specs=[SMEM, SMEM] + [VMEM] * 4,
        out_specs=VMEM,
        cost_estimate=FREE,
        compiler_params=params(8),
        name="widen",
    )(ids, pattern, same, *cross, wide_ready)
    y_shape = jax.ShapeDtypeStruct((tall, lanes), BF16)
    acc_shape = jax.ShapeDtypeStruct((tall, lanes), F32)
    spread, y0, acc2, acc_own = pl.pallas_call(
        early_kernel,
        out_shape=(placed[0], y_shape, acc_shape, acc_shape),
        in_specs=[SMEM, SMEM] + [VMEM] * 6,
        out_specs=(VMEM,) * 4,
        cost_estimate=cost(0),
        compiler_params=params(12),
        name="early",
    )(ids, pattern, same, ready, parent, z1, z2, sib(z2))
    q1, *_ = lax.optimization_barrier((q1, spread, y0, acc2, acc_own))
    q1_sib = sib(q1)
    acc13, q1 = pl.pallas_call(
        middle_kernel,
        out_shape=(jax.ShapeDtypeStruct((2 * tall, lanes), F32), jax.ShapeDtypeStruct(q1.shape, BF16)),
        in_specs=[SMEM] + [VMEM] * 4,
        out_specs=(VMEM, VMEM),
        cost_estimate=FREE,
        compiler_params=params(12),
        name="middle",
    )(ids, acc_own, sib(z1), spread, q1)
    q2, *_ = lax.optimization_barrier((q2, acc13))
    return pl.pallas_call(
        final_kernel,
        out_shape=(
            jax.ShapeDtypeStruct((children, rows, lane), BF16),
            jax.ShapeDtypeStruct((children, width, lane), BF16),
        ),
        in_specs=[SMEM, SMEM, SMEM] + [VMEM] * 10,
        out_specs=(VMEM, VMEM),
        scratch_shapes=[pltpu.VMEM((4 * tall, lanes), BF16)],
        cost_estimate=FREE,
        compiler_params=params(16),
        name="final",
    )(ids, pattern, widths, q1, q1_sib, q2, sib(q2), spread, full, y0, acc2, acc13, diag_inverse)


def solution(mesh):
    placed = (
        P(("pole", "row"), "col"),
        P(("pole", "row"), "col", None),
        P(("pole", "row"), None, "sub"),
        P("row", None),
        P("row"),
    )
    shape = dict(mesh.shape)
    fits = (shape["row"], shape["col"], shape["sub"]) == (4, 2, 2)
    return jax.shard_map(
        gathered if fits else generic,
        mesh=mesh,
        in_specs=placed,
        out_specs=(P(("pole", "row"), "col", "sub"), P(("pole", "row"), None, "sub")),
        check_vma=False,
    )
```
